32 devices in a mesh: node: 16 (over z, x, core), local: 2 (over y).
Axes of the slice: x: 2, y: 2, z: 4, core: 2. Of those that a mesh axis runs over, the one named last changes fastest.
Arguments:
- grad_values: bfloat16 [32, 8192, 512], P(('node', 'local')), may hold values from -1.75 to 1.75
- grad_exponents: int32 [32, 4, 8192], P(('node', 'local')), may hold values from -1 to 2
- proj: float32 [8192, 256], P(('local', 'node')), may hold values from -0.75 to 0.75
- weights: float32 [8192, 512], P(('local', 'node')), may hold values from -4 to 4
- moment1: float32 [256, 512], P('node'), may hold values from -6 to 6
- moment2: float32 [256, 512], P('node'), may hold values from 1 to 100
Outputs:
- quant_values: bfloat16 [8192, 512], P('local')
- quant_scales: bfloat16 [4, 8192], P(None, 'local')
- new_weights: float32 [8192, 512], P(('local', 'node'))
- new_moment1: float32 [256, 512], P('node')
- new_moment2: float32 [256, 512], P('node')
The draws below stay inside these ranges and needn't reach their ends.
All inputs are finite; a program needn't handle non-finite values. Where the reference program divides by a largest or mean magnitude, that divisor is 1e-20 or more.
Results may differ from the reference program's by a relative error of at most 0.0085.
Values may be sent and summed in bfloat16 or wider, within the bound.
No kernel may reach another device: no remote copies, remote signals or barrier semaphores. Data moves between devices by JAX's collectives and lax.ppermute only.
A program may use at most 128 MiB of HBM per device.

```python
import math
import jax
import jax.numpy as jnp
from jax import lax

D = 8192
COLS = 512
RANK = 256
BLOCK = 128
CB = 4
N_NODE = 16
N_LOCAL = 2


def set_ends(array, stream_key, smallest, high):
    shape = array.shape
    place = [jax.random.randint(jax.random.fold_in(stream_key, axis), (), 0, shape[axis]) for axis in range(len(shape))]
    array = array.at[tuple(place)].set(smallest)
    longest = shape.index(max(shape))
    place[longest] = (place[longest] + 1) % shape[longest]
    return array.at[tuple(place)].set(high)


def strengthened(drawn, rng, source, target, shards_of, factor):
    owner, partner = [(jnp.arange(drawn.shape[axis_at]) // (drawn.shape[axis_at] // shards_of)).reshape([-1 if axis == axis_at else 1 for axis in range(drawn.ndim)]) for axis_at in (source, target)]
    chosen = jax.random.permutation(rng, shards_of)[partner]
    strong = (owner == chosen) | (owner == (partner + shards_of // 2) % shards_of)
    return jnp.where(strong, factor * drawn, drawn)


def steps_of(key, shape, cuts, least, largest):
    def one(position, parts):
        heights = jax.random.uniform(jax.random.fold_in(jax.random.fold_in(key, 6), position), (parts,), jnp.float32, least / len(cuts), largest / len(cuts))
        return jnp.repeat(jnp.exp(heights), shape[position] // parts).reshape((-1,) + (1,) * (len(shape) - position - 1))

    loudness = one(*cuts[0])
    for cut in cuts[1:]:
        loudness = loudness * one(*cut)
    return loudness


def normal_values(own_key, dims, deviation, bound, pieces=(), held_as=jnp.bfloat16):
    drawn = jax.random.normal(own_key, dims, jnp.float32) * deviation
    if len(pieces) > 0:
        drawn = steps_of(own_key, dims, pieces, -0.22, 0.18) * drawn
    return jnp.clip(drawn, min=-bound, max=bound).astype(held_as)


def noise_with(own_key, dims, scale, most, pieces, heavy, held_as=jnp.bfloat16):
    entries = scale * jax.random.normal(own_key, dims, jnp.float32)
    if pieces:
        entries = entries * steps_of(own_key, dims, pieces, -0.22, 0.18)
    return jnp.clip(strengthened(entries, jax.random.fold_in(own_key, 3), *heavy), -most, most).astype(held_as)


def setup_inputs(seed: int = 0) -> dict:
    key_of = jax.random.split(jax.random.key(seed), 7)
    grad_values = noise_with(key_of[0], (N_NODE * N_LOCAL, D, COLS), 0.0625, 1.75, ((0, 32),), (0, 1, 32, 2.75))
    grad_exponents = set_ends(jax.random.randint(key_of[1], (N_NODE * N_LOCAL, CB, D), -1, 3), jax.random.fold_in(key_of[1], 1), -1, 2).astype(jnp.int32)
    proj = noise_with(key_of[2], (D, RANK), RANK ** -0.5, 0.75, ((0, 32),), (0, 1, 32, 2.75), jnp.float32)
    weights = normal_values(key_of[3], (D, COLS), 0.25, 4.0, ((0, 32),), jnp.float32)
    moment1 = normal_values(key_of[4], (RANK, COLS), 1.0, 6.0, ((0, 16),), jnp.float32)
    moment2 = jnp.clip(jnp.exp(math.log(100.0) - 4.6051702 * jax.random.uniform(key_of[5], (RANK, COLS), jnp.float32) ** steps_of(key_of[5], (RANK, COLS), ((0, 16),), -0.2, 0.2)), 1.0, 100.0)
    return dict(grad_values=grad_values, grad_exponents=grad_exponents, proj=proj, weights=weights, moment1=moment1, moment2=moment2)


bias_first = 1.0 - 0.9 ** 10
bias_second = 1.0 - 0.999 ** 10

def reference(grad_values, grad_exponents, proj, weights, moment1, moment2):

    def add_partial(index, total):
        mantissa = grad_values[index].astype(jnp.float32)
        factor = jnp.exp2(grad_exponents[index].astype(jnp.float32))
        scaled = mantissa.reshape(D, CB, BLOCK) * jnp.transpose(factor)[:, :, None]
        return total + scaled.reshape(D, COLS)
    grad = lax.fori_loop(0, N_NODE * N_LOCAL, add_partial, jnp.zeros((D, COLS), jnp.float32))
    projected = jnp.dot(jnp.transpose(proj), grad, precision=lax.Precision.HIGHEST, preferred_element_type=jnp.float32)
    new_moment1 = 0.9 * moment1 + 0.1 * projected
    new_moment2 = 0.999 * moment2 + 0.001 * projected * projected
    tilde = new_moment1 / bias_first / (jnp.sqrt(new_moment2 / bias_second) + 1e-08)
    col_scale = jnp.sqrt(lax.optimization_barrier(jnp.sum(tilde * tilde, 0))) / jnp.sqrt(lax.optimization_barrier(jnp.sum(projected * projected, 0)) + 1e-06)
    new_weights = weights - 8.0 * grad * col_scale[None, :]
    blocks = new_weights.reshape(D, CB, BLOCK)
    block_max = (lax.optimization_barrier(jnp.max(jnp.abs(blocks), 2)) + 1e-06).astype(jnp.bfloat16)
    quant_values = (blocks / block_max.astype(jnp.float32)[:, :, None]).reshape(D, COLS).astype(jnp.bfloat16)
    quant_scales = jnp.transpose(block_max)
    return (quant_values, quant_scales, new_weights, new_moment1, new_moment2)
```

```python
import functools

import jax
import jax.numpy as jnp
from jax import lax
from jax.experimental import pallas as pl
from jax.experimental.pallas import tpu as pltpu
from jax.sharding import PartitionSpec as P

f32, bf16 = jnp.float32, jnp.bfloat16
bias_first = 1.0 - 0.9**10
bias_second = 1.0 - 0.999**10
AXES = ("node", "local")
GROUPS = 2
PAD = 16
ALL = slice(None)
MIB = 2**20


def total(terms):
    return functools.reduce(lambda a, b: a + b, [t.astype(f32) for t in terms])


def at(array, index, axis):
    return lax.dynamic_index_in_dim(array, index, axis, False)


def vmem(array):
    return pltpu.with_memory_space_constraint(array, pltpu.VMEM)


def call(kernel, name, where, arrays, outs, scratch=(), limit=8, flops=0):
    nbytes = sum(a.size * a.dtype.itemsize for a in arrays)
    return pl.pallas_call(
        kernel,
        out_shape=outs,
        in_specs=[pl.BlockSpec(memory_space=pltpu.SMEM)]
        + [pl.BlockSpec(memory_space=pltpu.VMEM)] * len(arrays),
        out_specs=jax.tree.map(lambda _: pl.BlockSpec(memory_space=pltpu.VMEM), outs),
        scratch_shapes=scratch,
        compiler_params=pltpu.CompilerParams(vmem_limit_bytes=limit * MIB),
        cost_estimate=pl.CostEstimate(flops=flops, bytes_accessed=nbytes, transcendentals=0),
        name=name,
    )(where, *[vmem(a) for a in arrays])


def dequant(values, exponents, where, away, dims, blocksize, first, parts, part):
    cores, local, rest, pair, rows = dims
    nblocks = exponents.shape[0]
    columns = part * parts
    if rows % 128:
        which = lax.rem(where[2] + away, cores)
        power = jnp.exp2(exponents.astype(f32)).astype(bf16)
        picked = power.reshape(-1, local, rest, pair, cores, rows)
        picked = jnp.moveaxis(at(picked, which, 4), 0, -1)
        mant = at(values.reshape(local, rest, pair, cores, rows, -1, blocksize), which, 3)
        out = (mant * picked[..., None]).reshape(local, rest, pair, rows, -1)
        return [out[..., first + k * part : first + (k + 1) * part] for k in range(parts)]

    def kernel(where, exps, mant, *refs):
        outs, held, sems = refs[:parts], refs[parts], refs[parts + 1]
        which = lax.rem(where[2] + away, cores)
        copies = {}
        for l in range(local):
            for r in range(rest):
                copies[l, r] = pltpu.make_async_copy(
                    mant.at[l, r, :, which, :, pl.ds(first, columns)],
                    held.at[l, r],
                    sems.at[l, r],
                )
                copies[l, r].start()
        spread = lax.broadcasted_iota(jnp.int32, (nblocks, columns), 1) + first
        spread = spread // blocksize == lax.broadcasted_iota(jnp.int32, (nblocks, columns), 0)
        spread = spread.astype(bf16)
        for l in range(local):
            for r in range(rest):
                copies[l, r].wait()
                for i in range(pair):
                    start = (((l * rest + r) * pair + i) * cores + which) * rows
                    power = exps[:, pl.ds(pl.multiple_of(start, 128), rows)].astype(f32)
                    factor = lax.dot_general(
                        jnp.exp2(power).astype(bf16),
                        spread,
                        (((0,), (0,)), ((), ())),
                        preferred_element_type=f32,
                    )
                    scaled = (held[l, r, i].astype(f32) * factor).astype(bf16)
                    for k in range(parts):
                        outs[k][l, r, i] = scaled[:, k * part : (k + 1) * part]

    mant = values.reshape(local, rest, pair, cores, rows, -1)
    return pl.pallas_call(
        kernel,
        out_shape=[pltpu.VMEM((local, rest, pair, rows, part), bf16)] * parts,
        in_specs=[
            pl.BlockSpec(memory_space=pltpu.SMEM),
            pl.BlockSpec(memory_space=pltpu.VMEM),
            pl.BlockSpec(memory_space=pl.ANY),
        ],
        out_specs=[pl.BlockSpec(memory_space=pltpu.VMEM)] * parts,
        scratch_shapes=[
            pltpu.VMEM((local, rest, pair, rows, columns), bf16),
            pltpu.SemaphoreType.DMA((local, rest)),
        ],
        compiler_params=pltpu.CompilerParams(vmem_limit_bytes=16 * MIB),
        cost_estimate=pl.CostEstimate(
            flops=2 * values.size // cores,
            bytes_accessed=4 * values.shape[0] * columns // cores,
            transcendentals=0,
        ),
        name="dequant",
    )(where, vmem(exponents), pltpu.with_memory_space_constraint(mant, pltpu.HBM))


def fold(where, terms, shape):
    def kernel(where, *refs):
        place = [where[i] for i in range(4)]
        *arrays, out = refs
        out[...] = total([a[pick(*place)] for a, (_, pick) in zip(arrays, terms)]).astype(bf16)

    return call(kernel, "fold", where, [a for a, _ in terms], pltpu.VMEM(shape, bf16))


def project(where, first, second, packs, dims, ranks, nodes):
    cores, local, rest, pair, rows = dims
    half = first[0][0].shape[-1]
    group = 2 * half
    each = ranks // nodes

    def kernel(where, *refs):
        place = [where[i] for i in range(4)]
        arrays, refs = refs[: len(first) + len(second)], refs[len(first) + len(second) :]
        projs, refs = refs[:rest], refs[rest:]
        sends, outs, scratch = refs[:rest], refs[rest:-1], refs[-1]
        acc = None
        for d in range(rest):
            k = lax.rem(place[0] - d + rest, rest)
            for lo, terms, held in (
                (0, first, arrays[: len(first)]),
                (half, second, arrays[len(first) :]),
            ):
                parts = [a[pick(*place, k)] for a, (_, pick) in zip(held, terms)]
                sends[d][:, lo : lo + half] = total(parts).astype(bf16)
            term = lax.dot_general(
                projs[d][:rows], sends[d][...], (((0,), (0,)), ((), ())), preferred_element_type=f32
            )
            acc = term if acc is None else acc + term
        scratch[...] = acc.reshape(scratch.shape)
        for d, out in enumerate(outs):
            out[...] = scratch[:, lax.rem(place[2] + d, cores)].reshape(out.shape)

    out = call(
        kernel,
        "project",
        where,
        [a for a, _ in first + second] + packs,
        [pltpu.VMEM((rows, group), bf16)] * rest
        + [pltpu.VMEM((ranks // cores, group), f32)] * cores,
        [pltpu.VMEM((nodes // cores, cores, each, group), f32)],
        limit=12,
        flops=2 * rest * rows * ranks * group,
    )
    return out[:rest], out[rest:]


def add(where, terms, name):
    def kernel(where, *refs):
        *arrays, out = refs
        out[...] = total([a[...] for a in arrays]).astype(bf16)

    return call(kernel, name, where, terms, pltpu.VMEM(terms[0].shape, bf16))


def pack(where, proj, pairs):
    rows, ranks = proj.shape
    deep, columns = pairs[0].shape
    cuts = columns // ranks

    def kernel(where, *refs):
        proj, *pairs, out = refs
        out[:rows] = proj[...].astype(bf16)
        for j, held in enumerate(pairs):
            for h in range(cuts):
                start = rows + (j * cuts + h) * deep
                out[start : start + deep] = held[:, h * ranks : (h + 1) * ranks]

    shape = (rows + len(pairs) * cuts * deep, ranks)
    return call(kernel, "pack", where, [proj] + pairs, pltpu.VMEM(shape, bf16))


def normalize(where, parts, packs, dims, first, columns, nodes):
    cores, local, rest, pair, rows = dims
    ranks = packs[0].shape[1]
    group = parts[0].shape[1]
    each = ranks // nodes
    cuts = columns // ranks

    def kernel(where, *refs):
        z, x = where[0], where[1]
        arrays, held, (sums, mine, scratch) = refs[:rest], refs[rest : 2 * rest], refs[2 * rest :]
        scratch[...] = total([a[...] for a in arrays]).reshape(scratch.shape)
        mine[...] = scratch[z * pair + x]
        raw, tilde = 0.0, 0.0
        for dz in range(rest):
            for dx in range(pair):
                k = lax.rem(z - dz + rest, rest) * pair + lax.rem(x - dx + pair, pair)
                value = scratch[k]
                old = []
                for h in range(cuts):
                    start = rows + (dx * cuts + h) * 2 * each
                    old.append(held[dz][start : start + 2 * each].astype(f32))
                old = jnp.concatenate(old, 1)[:, first : first + group]
                m1 = 0.9 * old[:each] + 0.1 * value
                m2 = 0.999 * old[each:] + 0.001 * value * value
                ratio = m1 / bias_first / (jnp.sqrt(m2 / bias_second) + 1e-08)
                raw += jnp.sum(value * value, 0, keepdims=True)
                tilde += jnp.sum(ratio * ratio, 0, keepdims=True)
        sums[...] = jnp.concatenate([raw, tilde, jnp.zeros((6, group), f32)], 0)

    return call(
        kernel,
        "normalize",
        where,
        parts + packs,
        [pltpu.VMEM((8, group), f32), pltpu.VMEM((each, group), f32)],
        [pltpu.VMEM((rest * pair, each, group), f32)],
    )


def update(where, weights, moments, grads, sums, mines, blocksize):
    rows, columns = weights.shape
    count, each = len(grads), len(grads[0])
    group = columns // count

    def kernel(where, weights, moment1, moment2, *refs):
        grads, refs = refs[: count * each], refs[count * each :]
        sums, refs = refs[: count * len(sums_in[0])], refs[count * len(sums_in[0]) :]
        mines, (new_out, packed, new1, new2) = refs[:count], refs[count:]
        packed[rows:, :] = jnp.zeros((PAD, columns), bf16)
        lane = lax.broadcasted_iota(jnp.int32, (rows, 128), 1)
        scales = jnp.zeros((rows, 128), f32)
        for g in range(count):
            per = len(sums_in[0])
            added = total([s[...] for s in sums[g * per : (g + 1) * per]])
            col_scale = jnp.sqrt(added[1:2]) / jnp.sqrt(added[0:1] + 1e-06)
            for k in range(group // blocksize):
                inner = slice(k * blocksize, (k + 1) * blocksize)
                cols = slice(g * group + k * blocksize, g * group + (k + 1) * blocksize)
                grad = total([t[:, inner] for t in grads[g * each : (g + 1) * each]])
                new = weights[:, cols] - 8.0 * grad * col_scale[:, inner]
                new_out[:, cols] = new
                scale = (jnp.max(jnp.abs(new), 1, keepdims=True) + 1e-06).astype(bf16).astype(f32)
                packed[:rows, cols] = (new / scale).astype(bf16)
                scales = jnp.where(lane == g * (group // blocksize) + k, scale, scales)
            cols = slice(g * group, (g + 1) * group)
            mine = mines[g][...]
            new1[:, cols] = 0.9 * moment1[:, cols] + 0.1 * mine
            new2[:, cols] = 0.999 * moment2[:, cols] + 0.001 * mine * mine
        packed[rows:, :rows] = jnp.transpose(scales)[:PAD].astype(bf16)

    sums_in = sums
    return call(
        kernel,
        "update",
        where,
        [weights, *moments] + [t for g in grads for t in g] + [s for g in sums for s in g] + mines,
        [
            jax.ShapeDtypeStruct((rows, columns), f32),
            pltpu.VMEM((rows + PAD, columns), bf16),
            jax.ShapeDtypeStruct(moments[0].shape, f32),
            jax.ShapeDtypeStruct(moments[0].shape, f32),
        ],
    )


def lay(where, shards, places, nblocks):
    rows, columns = shards[0].shape[0] - PAD, shards[0].shape[1]
    count = len(shards)
    if rows % 128:
        places = jnp.stack([place(*[where[i] for i in range(4)]) for place in places])
        order = jnp.zeros(count, jnp.int32).at[places].set(jnp.arange(count, dtype=jnp.int32))
        stacked = jnp.take(jnp.stack(shards), order, axis=0)
        values = stacked[:, :rows].reshape(count * rows, columns)
        scales = jnp.moveaxis(stacked[:, rows : rows + nblocks, :rows], 0, 1)
        return values, scales.reshape(nblocks, count * rows)

    def kernel(where, *refs):
        held, (values, scales, sems) = refs[:count], refs[count:]
        place = [where[i] for i in range(4)]
        copies = []
        for k in range(count):
            start = pl.multiple_of(places[k](*place) * rows, 128)
            copies.append(
                pltpu.make_async_copy(
                    held[k].at[pl.ds(0, rows)], values.at[pl.ds(start, rows)], sems.at[k]
                )
            )
            copies[-1].start()
        for k in range(count):
            start = pl.multiple_of(places[k](*place) * rows, 128)
            tail = held[k][rows:, :rows].astype(f32)[:nblocks]
            scales[:, pl.ds(start, rows)] = tail.astype(bf16)
        for copy in copies:
            copy.wait()

    return pl.pallas_call(
        kernel,
        out_shape=[
            pltpu.HBM((count * rows, columns), bf16),
            jax.ShapeDtypeStruct((nblocks, count * rows), bf16),
        ],
        in_specs=[pl.BlockSpec(memory_space=pltpu.SMEM)]
        + [pl.BlockSpec(memory_space=pltpu.VMEM)] * count,
        out_specs=[pl.BlockSpec(memory_space=pl.ANY), pl.BlockSpec(memory_space=pltpu.VMEM)],
        scratch_shapes=[pltpu.SemaphoreType.DMA((count,))],
        compiler_params=pltpu.CompilerParams(vmem_limit_bytes=8 * MIB),
        cost_estimate=pl.CostEstimate(
            flops=0, bytes_accessed=4 * count * rows * columns, transcendentals=0
        ),
        name="lay",
    )(where, *[vmem(s) for s in shards])


def shards(grad_values, grad_exponents, proj, weights, moment1, moment2):
    nodes, local = lax.axis_size("node"), lax.axis_size("local")
    cores = 2 if nodes % 2 == 0 else 1
    pair = 2 if nodes // cores % 2 == 0 else 1
    rest = nodes // cores // pair
    node, y = lax.axis_index("node"), lax.axis_index("local")
    c, x, z = node % cores, node // cores % pair, node // cores // pair
    where = jnp.stack([z, x, c, y]).astype(jnp.int32)
    values, exponents = grad_values[0], grad_exponents[0]
    width, columns = values.shape
    nblocks = exponents.shape[0]
    blocksize = columns // nblocks
    rows = width // nodes // local
    ranks = proj.shape[1]
    dims = (cores, local, rest, pair, rows)

    def to(array, dz=0, dx=0, dc=0, dy=0):
        pairs = []
        for n in range(nodes):
            cc, xx, zz = n % cores, n // cores % pair, n // cores // pair
            there = ((zz + dz) % rest * pair + (xx + dx) % pair) * cores + (cc + dc) % cores
            for l in range(local):
                pairs.append((n * local + l, there * local + (l + dy) % local))
        return lax.ppermute(array, AXES, pairs)

    both = jnp.concatenate([moment1, moment2]).astype(bf16)
    packs = [pack(where, proj, [to(both, dx=d) if d else both for d in range(pair)])]
    packs += [to(packs[0], dz=d) for d in range(1, rest)]

    group = columns // GROUPS
    half = group // 2
    grads, sums, mines = [], [], []
    for g in range(GROUPS):
        cut = [[], []]
        for d in range(cores):
            for k, part in enumerate(
                dequant(values, exponents, where, d, dims, blocksize, g * group, 2, half)
            ):
                cut[k].append(to(part, dc=d) if d else part)
        first, second = cut

        over_x = []
        for d in range(1, pair):
            pick = lambda z, x, c, y, d=d: (ALL, ALL, lax.rem(x + d, pair))
            over_x.append(
                to(fold(where, [(t, pick) for t in first], (local, rest, rows, half)), dx=d)
            )
        over_y = []
        for d in range(1, local):
            pick = lambda z, x, c, y, d=d: (lax.rem(y + d, local), ALL, x)
            pick_x = lambda z, x, c, y, d=d: (lax.rem(y + d, local),)
            terms = [(t, pick) for t in first] + [(t, pick_x) for t in over_x]
            over_y.append(to(fold(where, terms, (rest, rows, half)), dy=d))
        first = (
            [(t, lambda z, x, c, y, k: (y, k, x)) for t in first]
            + [(t, lambda z, x, c, y, k: (y, k)) for t in over_x]
            + [(t, lambda z, x, c, y, k: (k,)) for t in over_y]
        )

        over_y = []
        for d in range(1, local):
            pick = lambda z, x, c, y, d=d: (lax.rem(y + d, local),)
            over_y.append(
                to(fold(where, [(t, pick) for t in second], (rest, pair, rows, half)), dy=d)
            )
        over_x = []
        for d in range(1, pair):
            pick = lambda z, x, c, y, d=d: (y, ALL, lax.rem(x + d, pair))
            pick_y = lambda z, x, c, y, d=d: (ALL, lax.rem(x + d, pair))
            terms = [(t, pick) for t in second] + [(t, pick_y) for t in over_y]
            over_x.append(to(fold(where, terms, (rest, rows, half)), dx=d))
        second = (
            [(t, lambda z, x, c, y, k: (y, k, x)) for t in second]
            + [(t, lambda z, x, c, y, k: (k, x)) for t in over_y]
            + [(t, lambda z, x, c, y, k: (k,)) for t in over_x]
        )

        parts, projected = project(where, first, second, packs, dims, ranks, nodes)
        grads.append([parts[0]] + [to(parts[rest - d], dz=d) for d in range(1, rest)])

        received = [to(projected[d], dc=d) for d in range(1, cores)]
        projected = add(where, [projected[0]] + received, "add_cores")
        by_y = []
        for dy in range(local):
            for dx in range(pair):
                by_y.append(to(projected, dx=dx, dy=dy) if dx or dy else projected)
        if local > 2:
            stacked = jnp.stack(by_y).reshape((local, pair) + projected.shape)
            stacked = jnp.take(stacked, (y - jnp.arange(local)) % local, axis=0)
            by_y = [stacked[i, j] for i in range(local) for j in range(pair)]
        projected = add_pairs(where, by_y, pair)
        projected = [projected] + [to(projected, dz=d) for d in range(1, rest)]
        added, mine = normalize(where, projected, packs, dims, g * group, columns, nodes)
        sums.append([added] + [to(added, dc=d) for d in range(1, cores)])
        mines.append(mine)

    new, packed, new1, new2 = update(
        where, weights, [moment1, moment2], grads, sums, mines, blocksize
    )

    held, places = [], []
    for dz in range(rest):
        for dx in range(pair):
            for dc in range(cores):
                if dc:
                    shard = to(held[-dc], dc=dc)
                elif dx:
                    shard = to(held[-dx * cores], dx=dx)
                else:
                    shard = to(packed, dz=dz) if dz else packed
                held.append(shard)

                def place(z, x, c, y, dz=dz, dx=dx, dc=dc):
                    zx = lax.rem(z - dz + rest, rest) * pair + lax.rem(x - dx + pair, pair)
                    return zx * cores + lax.rem(c - dc + cores, cores)

                places.append(place)
    quant, scales = lay(where, held, places, nblocks)
    return quant, scales, new, new1, new2


def add_pairs(where, terms, pair):
    def kernel(where, *refs):
        *arrays, out = refs
        runs = [total([a[...] for a in arrays[i : i + pair]]) for i in range(0, len(arrays), pair)]
        out[...] = total(runs).astype(bf16)

    return call(kernel, "add_chips", where, terms, pltpu.VMEM(terms[0].shape, bf16))


def solution(mesh):
    return jax.shard_map(
        shards,
        mesh=mesh,
        in_specs=(
            P(("node", "local"), None, None),
            P(("node", "local"), None, None),
            P(("local", "node"), None),
            P(("local", "node"), None),
            P("node", None),
            P("node", None),
        ),
        out_specs=(
            P("local", None),
            P(None, "local"),
            P(("local", "node"), None),
            P("node", None),
            P("node", None),
        ),
        check_vma=False,
    )
```

```python
import functools

import jax
import jax.numpy as jnp
from jax import lax
from jax.experimental import pallas as pl
from jax.experimental.pallas import tpu as pltpu
from jax.sharding import PartitionSpec as P

f32, bf16 = jnp.float32, jnp.bfloat16
bias_first = 1.0 - 0.9**10
bias_second = 1.0 - 0.999**10
AXES = ("node", "local")
KNOBS = {'orders': ('xyw', 'ywx', 'wxy', 'xyw'), 'plan': ('0x', '1y', '2w', 'pack', '3x', '0y', '1w', '2x', '3y', '0w', '1x', '2y', '3w'), 'cost': {}, 'turn': False, 'late': (), 'early': False, 'sums': 1, 'cube': False, 'ag': {'lays': 2, 'ties': (), 'halves': False}}
ORDERS = KNOBS["orders"]
PLAN = KNOBS["plan"]
COST = KNOBS["cost"]
TIES = [tuple(t) for t in KNOBS["ag"]["ties"]]
PAD = 16
ALL = slice(None)
MIB = 2**20


def total(terms):
    return functools.reduce(lambda a, b: a + b, [t.astype(f32) for t in terms])


def at(array, index, axis):
    return lax.dynamic_index_in_dim(array, index, axis, False)


def vmem(array):
    return pltpu.with_memory_space_constraint(array, pltpu.VMEM)


class Grid:
    def __init__(self):
        nodes, local = lax.axis_size("node"), lax.axis_size("local")
        size, left = {"y": local}, nodes
        for axis in "cxw":
            size[axis] = 2 if left % 2 == 0 else 1
            left //= size[axis]
        size["v"] = left
        self.size, self.nodes = size, nodes

    def split(self, node):
        place = {}
        for axis in "cxwv":
            place[axis], node = node % self.size[axis], node // self.size[axis]
        return place

    def node(self, place):
        node = 0
        for axis in "vwxc":
            node = node * self.size[axis] + place[axis]
        return node

    def place(self):
        place, node = {"y": lax.axis_index("local")}, lax.axis_index("node")
        for axis in "cxwv":
            place[axis] = lax.rem(node, self.size[axis])
            node = lax.div(node, self.size[axis])
        return place

    def step(self, axis, here, d):
        size = self.size[axis]
        if size & (size - 1):
            if isinstance(here, int):
                return (here + d) % size
            return lax.rem(here + (d + size) % size, size)
        if isinstance(here, int):
            return here ^ abs(d)
        return lax.bitwise_xor(here, jnp.int32(abs(d)))

    def others(self, axis):
        return range(1, self.size[axis])

    def send(self, array, **steps):
        local, pairs = self.size["y"], []
        for n in range(self.nodes):
            for y in range(local):
                place = self.split(n) | {"y": y}
                there = {a: self.step(a, i, steps.get(a, 0)) for a, i in place.items()}
                pairs.append((n * local + y, self.node(there) * local + there["y"]))
        return lax.ppermute(array, AXES, pairs)


class Turn:
    last = None


def touch(*arrays):
    def kernel(out):
        out[...] = jnp.zeros((8, 128), f32)

    return call(kernel, "touch", [], pltpu.VMEM((8, 128), f32), extra=arrays)


def tie(array, *others):
    return pl.pallas_call(
        lambda *refs: None,
        out_shape=pltpu.VMEM(array.shape, array.dtype),
        in_specs=[pl.BlockSpec(memory_space=pl.ANY)] * (1 + len(others)),
        out_specs=pl.BlockSpec(memory_space=pl.ANY),
        input_output_aliases={0: 0},
        cost_estimate=pl.CostEstimate(flops=0, bytes_accessed=1, transcendentals=0),
        name="tie",
    )(vmem(array), *[vmem(a) for a in others])


def call(kernel, name, arrays, outs, scratch=(), limit=8, extra=()):
    after = list(extra)
    if Turn.last is not None and KNOBS["turn"]:
        after.append(Turn.last)
    count, more = len(arrays), len(after)

    def body(*refs):
        kernel(*refs[:count], *refs[count + more :])

    arrays = list(arrays) + after
    out = pl.pallas_call(
        body,
        out_shape=outs,
        in_specs=[pl.BlockSpec(memory_space=pltpu.VMEM)] * count
        + [pl.BlockSpec(memory_space=pl.ANY)] * more,
        out_specs=jax.tree.map(lambda _: pl.BlockSpec(memory_space=pltpu.VMEM), outs),
        scratch_shapes=scratch,
        compiler_params=pltpu.CompilerParams(vmem_limit_bytes=limit * MIB),
        cost_estimate=pl.CostEstimate(flops=0, bytes_accessed=COST.get(name[:4], 1), transcendentals=0),
        name=name,
    )(*[vmem(a) for a in arrays])
    Turn.last = jax.tree.leaves(out)[-1]
    return out


def dequant(grid, values, exponents, away, rows, blocksize, parts):
    cores, local, pair = (grid.size[a] for a in "cyx")
    rest = grid.size["v"] * grid.size["w"]
    shape = tuple(grid.size[a] for a in "yvwx") + (rows, values.shape[1] // parts)
    nblocks, columns = exponents.shape[0], values.shape[1]
    part = columns // parts
    if rows % 128:
        which = grid.step("c", grid.place()["c"], away)
        power = jnp.exp2(exponents.astype(f32)).astype(bf16)
        picked = power.reshape(-1, local, rest, pair, cores, rows)
        picked = jnp.moveaxis(at(picked, which, 4), 0, -1)
        mant = at(values.reshape(local, rest, pair, cores, rows, -1, blocksize), which, 3)
        out = (mant * picked[..., None]).reshape(local, rest, pair, rows, -1)
        return [out[..., k * part : (k + 1) * part].reshape(shape) for k in range(parts)]

    def kernel(exps, mant, *refs):
        outs, (held, sems) = refs[:parts], refs[parts:]
        which = grid.step("c", grid.place()["c"], away)
        copies = {}
        for l in range(local):
            for r in range(rest):
                copies[l, r] = pltpu.make_async_copy(
                    mant.at[l, r, :, which], held.at[l, r], sems.at[l, r]
                )
                copies[l, r].start()
        spread = lax.broadcasted_iota(jnp.int32, (nblocks, columns), 1) // blocksize
        spread = spread == lax.broadcasted_iota(jnp.int32, (nblocks, columns), 0)
        spread = spread.astype(bf16)
        for l in range(local):
            for r in range(rest):
                copies[l, r].wait()
                for i in range(pair):
                    start = (((l * rest + r) * pair + i) * cores + which) * rows
                    power = exps[:, pl.ds(pl.multiple_of(start, 128), rows)].astype(f32)
                    factor = lax.dot_general(
                        jnp.exp2(power).astype(bf16),
                        spread,
                        (((0,), (0,)), ((), ())),
                        preferred_element_type=f32,
                    )
                    scaled = (held[l, r, i].astype(f32) * factor).astype(bf16)
                    for k in range(parts):
                        outs[k][l, r // shape[2], r % shape[2], i] = scaled[
                            :, k * part : (k + 1) * part
                        ]

    mant = values.reshape(local, rest, pair, cores, rows, columns)
    return pl.pallas_call(
        kernel,
        out_shape=[pltpu.VMEM(shape, bf16)] * parts,
        in_specs=[
            pl.BlockSpec(memory_space=pltpu.VMEM),
            pl.BlockSpec(memory_space=pl.ANY),
        ],
        out_specs=[pl.BlockSpec(memory_space=pltpu.VMEM)] * parts,
        scratch_shapes=[
            pltpu.VMEM((local, rest, pair, rows, columns), bf16),
            pltpu.SemaphoreType.DMA((local, rest)),
        ],
        compiler_params=pltpu.CompilerParams(vmem_limit_bytes=16 * MIB),
        cost_estimate=pl.CostEstimate(flops=0, bytes_accessed=1, transcendentals=0),
        name="dequant",
    )(vmem(exponents), pltpu.with_memory_space_constraint(mant, pltpu.HBM))


class Unit:
    def __init__(self, grid, terms):
        self.grid, self.left = grid, "yvwx"
        self.terms = [(t, "yvwx") for t in terms]

    @staticmethod
    def entry(axes, where):
        return tuple(where.get(a, ALL) for a in axes)

    def hop(self, axis):
        grid, left = self.grid, self.left.replace(axis, "")
        arrays = [t for t, _ in self.terms]
        shape = tuple(grid.size[a] for a in left) + arrays[0].shape[-2:]

        def kernel(*refs):
            held, outs = refs[: len(arrays)], refs[len(arrays) :]
            place = grid.place()
            for d, out in zip(grid.others(axis), outs):
                where = {a: i for a, i in place.items() if a not in self.left}
                where[axis] = grid.step(axis, place[axis], d)
                parts = [t[self.entry(axes, where)] for t, (_, axes) in zip(held, self.terms)]
                out[...] = total(parts).astype(bf16)

        outs = [pltpu.VMEM(shape, bf16) for _ in grid.others(axis)]
        if outs:
            outs = call(kernel, "fold_" + axis, arrays, outs)
        self.left = left
        for d, out in zip(grid.others(axis), outs):
            self.terms.append((grid.send(out, **{axis: d}), left))


def send_rows(grid, units):
    rows, part = units[0].terms[0][0].shape[-2:]
    arrays = [t for u in units for t, _ in u.terms]

    def kernel(*refs):
        held, outs = iter(refs[: len(arrays)]), refs[len(arrays) :]
        place = grid.place()
        for i, unit in enumerate(units):
            terms = [(next(held), axes) for _, axes in unit.terms]
            for d, out in zip(grid.others("v"), outs):
                where = place | {"v": grid.step("v", place["v"], d)}
                value = total([t[Unit.entry(axes, where)] for t, axes in terms])
                out[:, i * part : (i + 1) * part] = value.astype(bf16)

    outs = [pltpu.VMEM((rows, part * len(units)), bf16) for _ in grid.others("v")]
    outs = call(kernel, "fold_v", arrays, outs) if outs else outs
    return [grid.send(t, v=d) for d, t in zip(grid.others("v"), outs)]


def project(grid, units, packs, ranks, sent):
    size = grid.size
    rows, part = units[0].terms[0][0].shape[-2:]
    each = ranks // grid.nodes
    group = part * len(units)
    arrays = [t for u in units for t, _ in u.terms]
    late = [i for i in range(len(units)) if i not in sent]
    n_sends = size["v"] - 1 if late else 0

    def kernel(*refs):
        held, refs = iter(refs[: len(arrays)]), refs[len(arrays) :]
        projs, refs = refs[: size["v"]], refs[size["v"] :]
        own, later, refs = refs[0], refs[1 : 1 + n_sends], refs[1 + n_sends :]
        outs, acc, sends = refs[: size["c"]], refs[size["c"]], refs[size["c"] + 1 :]
        sends = [own, *sends]
        place = grid.place()
        dims = (((0,), (0,)), ((), ()))
        for i, unit in enumerate(units):
            terms = [(next(held), axes) for _, axes in unit.terms]
            cols = slice(i * part, (i + 1) * part)
            for d in range(size["v"]):
                where = place | {"v": grid.step("v", place["v"], d)}
                value = total([t[Unit.entry(axes, where)] for t, axes in terms])
                sends[d][:, cols] = value.astype(bf16)
                if d and i in late:
                    j = late.index(i)
                    later[d - 1][:, j * part : (j + 1) * part] = value.astype(bf16)
        sums = [
            lax.dot_general(came[:rows], send[...], dims, preferred_element_type=f32)
            for came, send in zip(projs, sends)
        ]
        acc[...] = total(sums)
        for d, out in enumerate(outs):
            core = grid.step("c", place["c"], d)
            for e in range(size["x"]):
                for f in range(size["w"]):
                    there = {"c": core, "x": grid.step("x", place["x"], e)}
                    there["w"] = grid.step("w", place["w"], f)
                    for v in range(size["v"]):
                        start = pl.multiple_of(grid.node(there | {"v": v}) * each, each)
                        out[e, f, v * each : (v + 1) * each] = acc[pl.ds(start, each)]

    out = call(
        kernel,
        "project",
        arrays + packs,
        [pltpu.VMEM((rows, group), bf16)]
        + [pltpu.VMEM((rows, part * len(late)), bf16)] * n_sends
        + [pltpu.VMEM((size["x"], size["w"], size["v"] * each, group), f32)] * size["c"],
        [pltpu.VMEM((ranks, group), f32)] + [pltpu.VMEM((rows, group), bf16)] * (size["v"] - 1),
        limit=12,
    )
    return out[0], out[1 : 1 + n_sends], out[1 + n_sends :]


def add_cut(terms, name, run=1, flat=False):
    if flat:
        return add_flat(terms, name)
    count = terms[0].shape[0]

    def kernel(*refs):
        arrays, outs = refs[: len(terms)], refs[len(terms) :]
        for e, out in enumerate(outs):
            parts = [a[e] for a in arrays]
            runs = [total(parts[i : i + run]) for i in range(0, len(parts), run)]
            out[...] = total(runs).astype(out.dtype)

    return call(kernel, name, terms, [pltpu.VMEM(terms[0].shape[1:], bf16)] * count)


def add_flat(terms, name):
    pair, wide = terms[0].shape[:2]

    def kernel(*refs):
        arrays, outs = refs[: len(terms)], refs[len(terms) :]
        for k, out in enumerate(outs):
            out[...] = total([a[k // wide, k % wide] for a in arrays]).astype(out.dtype)

    outs = [pltpu.VMEM(terms[0].shape[2:], bf16)] * (pair * wide)
    return call(kernel, name, terms, outs)


def add_runs(terms, name, run):
    def kernel(*refs):
        *arrays, out = refs
        runs = [total([a[...] for a in arrays[i : i + run]]) for i in range(0, len(arrays), run)]
        out[...] = total(runs).astype(bf16)

    return call(kernel, name, terms, pltpu.VMEM(terms[0].shape, bf16))


def add(terms, name, dtype):
    def kernel(*refs):
        *arrays, out = refs
        out[...] = total([a[...] for a in arrays]).astype(dtype)

    return call(kernel, name, terms, pltpu.VMEM(terms[0].shape, dtype))


def pack(proj, moments):
    rows, ranks = proj.shape
    each, columns = moments[0].shape
    cuts = columns // ranks

    def kernel(proj, moment1, moment2, out):
        out[:rows] = proj[...].astype(bf16)
        both = jnp.concatenate([moment1[...], moment2[...]], 0).astype(bf16)
        for h in range(cuts):
            start = rows + h * 2 * each
            out[start : start + 2 * each] = both[:, h * ranks : (h + 1) * ranks]

    shape = (rows + cuts * 2 * each, ranks)
    return call(kernel, "pack", [proj, *moments], pltpu.VMEM(shape, bf16))


def normalize(grid, parts, packs, rows, first, columns, extra=()):
    ranks = packs[0].shape[1]
    group = parts[0].shape[1]
    each = ranks // grid.nodes
    cuts = columns // ranks
    rest = grid.size["v"]

    def kernel(*refs):
        v = grid.place()["v"]
        arrays, held, (sums, mine, scratch) = refs[:rest], refs[rest : 2 * rest], refs[2 * rest :]
        scratch[...] = total([a[...] for a in arrays]).reshape(scratch.shape)
        mine[...] = scratch[v]
        raw, tilde = 0.0, 0.0
        for d in range(rest):
            value = scratch[grid.step("v", v, d)]
            old = []
            for h in range(cuts):
                start = rows + h * 2 * each
                old.append(held[d][start : start + 2 * each].astype(f32))
            old = jnp.concatenate(old, 1)[:, first : first + group]
            m1 = 0.9 * old[:each] + 0.1 * value
            m2 = 0.999 * old[each:] + 0.001 * value * value
            ratio = m1 / bias_first / (jnp.sqrt(m2 / bias_second) + 1e-08)
            raw += jnp.sum(value * value, 0, keepdims=True)
            tilde += jnp.sum(ratio * ratio, 0, keepdims=True)
        sums[...] = jnp.concatenate([raw, tilde, jnp.zeros((6, group), f32)], 0)

    return call(
        kernel,
        "normalize",
        parts + packs,
        [pltpu.VMEM((8, group), f32), pltpu.VMEM((each, group), f32)],
        [pltpu.VMEM((rest, each, group), f32)],
        extra=extra,
    )


def update(weights, moments, grads, sums, mine, blocksize):
    rows, columns = weights.shape
    halved = KNOBS["ag"]["halves"] and rows % 256 == 0

    def kernel(weights, moment1, moment2, *refs):
        grad_refs, refs = refs[: len(grads)], refs[len(grads) :]
        sum_refs, refs = refs[: len(sums)], refs[len(sums) :]
        mine, new_out, new1, new2, packed, *halves = refs
        packed[rows:, :] = jnp.zeros((PAD, columns), bf16)
        lane = lax.broadcasted_iota(jnp.int32, (rows, 128), 1)
        scales = jnp.zeros((rows, 128), f32)
        added = total([s[...] for s in sum_refs])
        col_scale = jnp.sqrt(added[1:2]) / jnp.sqrt(added[0:1] + 1e-06)
        for k in range(columns // blocksize):
            cols = slice(k * blocksize, (k + 1) * blocksize)
            parts = []
            for ref, (_, blocks) in zip(grad_refs, grads):
                for lo, there, width in blocks:
                    if lo <= cols.start < lo + width:
                        start = there + cols.start - lo
                        parts.append(ref[:, start : start + blocksize])
            grad = total(parts)
            new = weights[:, cols] - 8.0 * grad * col_scale[:, cols]
            new_out[:, cols] = new
            scale = (jnp.max(jnp.abs(new), 1, keepdims=True) + 1e-06).astype(bf16).astype(f32)
            packed[:rows, cols] = (new / scale).astype(bf16)
            scales = jnp.where(lane == k, scale, scales)
        new1[...] = 0.9 * moment1[...] + 0.1 * mine[...]
        new2[...] = 0.999 * moment2[...] + 0.001 * mine[...] * mine[...]
        packed[rows:, :rows] = jnp.transpose(scales)[:PAD].astype(bf16)
        for i, half in enumerate(halves):
            half[...] = packed[i * rows // 2 : i * rows // 2 + half.shape[0]]

    return call(
        kernel,
        "update",
        [weights, *moments, *[g for g, _ in grads], *sums, mine],
        [
            jax.ShapeDtypeStruct((rows, columns), f32),
            jax.ShapeDtypeStruct(moments[0].shape, f32),
            jax.ShapeDtypeStruct(moments[0].shape, f32),
            pltpu.VMEM((rows + PAD, columns), bf16),
        ]
        + [pltpu.VMEM((rows // 2 + i * PAD, columns), bf16) for i in range(2) if halved],
    )


def lay(grid, held, nblocks, whole, *begun):
    shards = [t[0] for t in held]
    spans = [t[1:4] for t in held]
    steps = [t[4] for t in held]
    columns, count = shards[0].shape[1], len(shards)
    rows = max(lo + n for lo, n, _ in spans)

    def node_of(k):
        place = grid.place()
        return grid.node({a: grid.step(a, place[a], -steps[k].get(a, 0)) for a in "vwxc"})

    if rows % 128:
        places = jnp.stack([node_of(k) for k in range(count)])
        order = jnp.zeros(count, jnp.int32).at[places].set(jnp.arange(count, dtype=jnp.int32))
        stacked = jnp.take(jnp.stack(shards), order, axis=0)
        values = stacked[:, :rows].reshape(count * rows, columns)
        scales = jnp.moveaxis(stacked[:, rows : rows + nblocks, :rows], 0, 1)
        return values, scales.reshape(nblocks, count * rows)

    def kernel(*refs):
        held, (values, scales, sems) = refs[:count], refs[count + len(begun) :]
        copies = []
        for k, (lo, n, _) in enumerate(spans):
            start = pl.multiple_of(node_of(k) * rows + lo, 128)
            copies.append(
                pltpu.make_async_copy(
                    held[k].at[pl.ds(0, n)], values.at[pl.ds(start, n)], sems.at[k]
                )
            )
            copies[-1].start()
        for k, (lo, n, full) in enumerate(spans):
            if full:
                start = pl.multiple_of(node_of(k) * rows, 128)
                tail = held[k][n:, :rows].astype(f32)[:nblocks]
                scales[:, pl.ds(start, rows)] = tail.astype(bf16)
        for copy in copies:
            copy.wait()

    return pl.pallas_call(
        kernel,
        out_shape=[
            pltpu.HBM((whole * rows, columns), bf16),
            pltpu.VMEM((nblocks, whole * rows), bf16),
        ],
        in_specs=[pl.BlockSpec(memory_space=pltpu.VMEM)] * count
        + [pl.BlockSpec(memory_space=pl.ANY), pl.BlockSpec(memory_space=pltpu.VMEM)][: len(begun)],
        input_output_aliases={count + i: i for i in range(len(begun))},
        out_specs=[pl.BlockSpec(memory_space=pl.ANY), pl.BlockSpec(memory_space=pltpu.VMEM)],
        scratch_shapes=[pltpu.SemaphoreType.DMA((count,))],
        compiler_params=pltpu.CompilerParams(vmem_limit_bytes=8 * MIB),
        cost_estimate=pl.CostEstimate(
            flops=0, bytes_accessed=COST.get("lay", 1), transcendentals=0
        ),
        name="lay",
    )(*[vmem(s) for s in shards], *begun)


def shards(grad_values, grad_exponents, proj, weights, moment1, moment2):
    grid = Grid()
    size = grid.size
    values, exponents = grad_values[0], grad_exponents[0]
    width, columns = values.shape
    nblocks = exponents.shape[0]
    blocksize = columns // nblocks
    rows = width // grid.nodes // size["y"]
    ranks = proj.shape[1]
    parts = len(ORDERS)

    other = dequant(grid, values, exponents, 1, rows, blocksize, parts) if size["c"] > 1 else []
    other = [grid.send(t, c=1) for t in other]
    mine = dequant(grid, values, exponents, 0, rows, blocksize, parts)
    units = [Unit(grid, list(terms)) for terms in zip(mine, *([other] if other else []))]
    Turn.last = None
    received, sent, part = [], [], columns // parts
    for turn in PLAN:
        if turn == "touch":
            touch(*packs[1:])
        elif turn[0] == "t":
            touch(*[t for i in turn[1:] for t, _ in units[int(i)].terms[-1:]])
        elif turn[0] == "b":
            chosen = [int(i) for i in turn[1:]]
            blocks = [(i * part, k * part, part) for k, i in enumerate(chosen)]
            received += [(t, blocks) for t in send_rows(grid, [units[i] for i in chosen])]
            sent += chosen
        elif turn == "pack":
            packs = [pack(proj, [moment1, moment2])]
            packs += [grid.send(packs[0], v=-d) for d in grid.others("v")]
        else:
            units[int(turn[0])].hop(turn[1])

    own, sends, projected = project(grid, units, packs, ranks, sent)
    blocks = [(i * part, k * part, part) for k, i in enumerate(i for i in range(parts) if i not in sent)]
    if "bulk" not in KNOBS["late"]:
        received += [(grid.send(t, v=d), blocks) for d, t in zip(grid.others("v"), sends)]

    terms = [projected[0]] + [grid.send(projected[d], c=d) for d in grid.others("c")]
    by_x = add_cut(terms, "add_cores", flat=KNOBS["cube"])
    by_y = []
    for dy in range(size["y"]):
        for dx in range(size["x"]):
            for dw in range(size["w"] if KNOBS["cube"] else 1):
                piece = by_x[dx * size["w"] + dw] if KNOBS["cube"] else by_x[dx]
                by_y.append(grid.send(piece, x=dx, y=dy, w=dw) if dx or dy or dw else piece)
    if size["y"] > 2:
        stacked = jnp.stack(by_y).reshape((size["y"], -1) + by_y[0].shape)
        came = jnp.stack([grid.step("y", grid.place()["y"], -d) for d in range(size["y"])])
        order = jnp.zeros(size["y"], jnp.int32).at[came].set(jnp.arange(size["y"], dtype=jnp.int32))
        stacked = jnp.take(stacked, order, axis=0)
        by_y = [stacked[i, j] for i in range(size["y"]) for j in range(stacked.shape[1])]
    if KNOBS["cube"]:
        by_w = [add_runs(by_y, "add_chips", len(by_y) // size["y"])]
    else:
        by_w = add_cut(by_y, "add_chips", size["x"])
    if "bulk" in KNOBS["late"]:
        received += [(grid.send(tie(t, by_w[0]), v=d), blocks) for d, t in zip(grid.others("v"), sends)]
    summed = by_w[0]
    if not KNOBS["cube"]:
        received_w = [grid.send(by_w[d], w=d) for d in grid.others("w")]
        summed = add([by_w[0]] + received_w, "add_w", bf16)
    summed = [summed] + [grid.send(summed, v=d) for d in grid.others("v")]
    extra = [t for t, _ in received] if KNOBS["early"] else []
    added, kept = normalize(grid, summed, packs, rows, 0, columns, extra)
    if KNOBS["sums"] == 0:
        sums = [added] + [
            grid.send(added, x=dx, w=dw)
            for dx in range(size["x"])
            for dw in range(size["w"])
            if dx or dw
        ]
        added = add(sums, "add_sums", f32)
        sums = [added] + [grid.send(added, c=d) for d in grid.others("c")]
    else:
        added = add([added] + [grid.send(added, c=d) for d in grid.others("c")], "add_sums", f32)
        sums = [added] + [
            grid.send(added, x=dx, w=dw)
            for dx in range(size["x"])
            for dw in range(size["w"])
            if dx or dw
        ]
    new, new1, new2, *packed = update(
        weights, [moment1, moment2], [(own, [(0, 0, columns)]), *received], sums, kept, blocksize
    )

    ag = KNOBS["ag"]
    whole = (packed[0], 0, rows, True)
    halves = [whole]
    if len(packed) > 1:
        halves = [(packed[1], 0, rows // 2, False), (packed[2], rows // 2, rows // 2, True)]

    def sent(shards, **step):
        return [(grid.send(t, **step), *rest) for t, *rest in shards]

    def tied(shards, *others):
        return [(tie(t, *others), *rest) for t, *rest in shards]

    first = {d: sent(halves, v=d) if d else [whole] for d in range(size["v"])}
    stages = [[(0, d) for d in range(size["w"])]]
    stages += [[(d, 0) for d in grid.others("v")]]
    stages += [[(d, e) for d in grid.others("v") for e in grid.others("w")]]
    came = {(d, e): sent(first[d], w=e) if e else first[d] for s in stages for d, e in s}
    done, count, over = [], grid.nodes, []
    for k, stage in enumerate(stages):
        held = []
        for dv, dw in stage:
            shards = came[dv, dw]
            if (k, 0) in TIES and done:
                shards = tied(shards, done[-1][1])
            if (k, 1) in TIES and len(done) > 1:
                shards = tied(shards, done[-2][1])
            if (k, 2) in TIES and over:
                shards = tied(shards, over[-1])
            for dx in range(size["x"]):
                moved = sent(shards, x=dx) if dx else shards
                if dx:
                    over.append(moved[-1][0])
                    if (k, 3) in TIES and done:
                        moved = tied(moved, done[-1][1])
                for dc in range(size["c"]):
                    there = {"v": dv, "w": dw, "x": dx, "c": dc}
                    held += [(*t, there) for t in (sent(moved, c=dc) if dc else moved)]
        done.append(held)
        if (ag["lays"] == 1 or rows % 128) and k < len(stages) - 1:
            continue
        if ag["lays"] == 2 and k == 0:
            continue
        held = [t for h in done if isinstance(h, list) for t in h]
        if not held:
            continue
        begun = [h for h in done if not isinstance(h, list)][-1:]
        result = lay(grid, held, nblocks, count, *(begun[0] if begun else ()))
        done = [h for h in done if not isinstance(h, list)] + [result]
    quant, scales = done[-1]
    return quant, scales, new, new1, new2


def solution(mesh):
    return jax.shard_map(
        shards,
        mesh=mesh,
        in_specs=(
            P(("node", "local"), None, None),
            P(("node", "local"), None, None),
            P(("local", "node"), None),
            P(("local", "node"), None),
            P("node", None),
            P("node", None),
        ),
        out_specs=(
            P("local", None),
            P(None, "local"),
            P(("local", "node"), None),
            P("node", None),
            P("node", None),
        ),
        check_vma=False,
    )
```

```python
import functools

import jax
import jax.numpy as jnp
from jax import lax
from jax.experimental import pallas as pl
from jax.experimental.pallas import tpu as pltpu
from jax.sharding import PartitionSpec as P

f32, bf16 = jnp.float32, jnp.bfloat16
bias_first = 1.0 - 0.9**10
bias_second = 1.0 - 0.999**10
AXES = ("node", "local")
PIECES = ((0, 4, 0, 1), (1, 4, 0, 1), (2, 4, 0, 1), (3, 4, 0, 2), (3, 4, 1, 2))
ORDERS = ("xyw", "ywx", "wxy", "ywx", "wxy")
PAD = 16
ALL = slice(None)
MIB = 2**20


def total(terms):
    return functools.reduce(lambda a, b: a + b, [t.astype(f32) for t in terms])


def at(array, index, axis):
    return lax.dynamic_index_in_dim(array, index, axis, False)


def vmem(array):
    return pltpu.with_memory_space_constraint(array, pltpu.VMEM)


class Grid:
    def __init__(self):
        nodes, local = lax.axis_size("node"), lax.axis_size("local")
        size, left = {"y": local}, nodes
        for axis in "cxw":
            size[axis] = 2 if left % 2 == 0 else 1
            left //= size[axis]
        size["v"] = left
        self.size, self.nodes = size, nodes

    def split(self, node):
        place = {}
        for axis in "cxwv":
            place[axis], node = node % self.size[axis], node // self.size[axis]
        return place

    def node(self, place):
        node = 0
        for axis in "vwxc":
            node = node * self.size[axis] + place[axis]
        return node

    def place(self):
        place, node = {"y": lax.axis_index("local")}, lax.axis_index("node")
        for axis in "cxwv":
            place[axis] = lax.rem(node, self.size[axis])
            node = lax.div(node, self.size[axis])
        return place

    def step(self, axis, here, d):
        size = self.size[axis]
        if size & (size - 1):
            if isinstance(here, int):
                return (here + d) % size
            return lax.rem(here + (d + size) % size, size)
        if isinstance(here, int):
            return here ^ abs(d)
        return lax.bitwise_xor(here, jnp.int32(abs(d)))

    def others(self, axis):
        return range(1, self.size[axis])

    def send(self, array, **steps):
        local, pairs = self.size["y"], []
        for n in range(self.nodes):
            for y in range(local):
                place = self.split(n) | {"y": y}
                there = {a: self.step(a, i, steps.get(a, 0)) for a, i in place.items()}
                pairs.append((n * local + y, self.node(there) * local + there["y"]))
        return lax.ppermute(array, AXES, pairs)


def call(kernel, name, arrays, outs, scratch=(), limit=8):
    return pl.pallas_call(
        kernel,
        out_shape=outs,
        in_specs=[pl.BlockSpec(memory_space=pltpu.VMEM)] * len(arrays),
        out_specs=jax.tree.map(lambda _: pl.BlockSpec(memory_space=pltpu.VMEM), outs),
        scratch_shapes=scratch,
        compiler_params=pltpu.CompilerParams(vmem_limit_bytes=limit * MIB),
        cost_estimate=pl.CostEstimate(flops=0, bytes_accessed=1, transcendentals=0),
        name=name,
    )(*[vmem(a) for a in arrays])


def dequant(grid, values, exponents, away, rows, blocksize, pieces):
    cores, local, pair = (grid.size[a] for a in "cyx")
    rest = grid.size["v"] * grid.size["w"]
    lead, parts = tuple(grid.size[a] for a in "yvwx"), len(pieces)
    shapes = [lead + (p[0].stop - p[0].start, p[1].stop - p[1].start) for p in pieces]
    nblocks, columns = exponents.shape[0], values.shape[1]
    if rows % 128:
        which = grid.step("c", grid.place()["c"], away)
        power = jnp.exp2(exponents.astype(f32)).astype(bf16)
        picked = power.reshape(-1, local, rest, pair, cores, rows)
        picked = jnp.moveaxis(at(picked, which, 4), 0, -1)
        mant = at(values.reshape(local, rest, pair, cores, rows, -1, blocksize), which, 3)
        out = (mant * picked[..., None]).reshape(lead + (rows, columns))
        return [out[(..., *p)] for p in pieces]

    def kernel(exps, mant, *refs):
        outs, (held, sems) = refs[:parts], refs[parts:]
        which = grid.step("c", grid.place()["c"], away)
        copies = {}
        for l in range(local):
            for r in range(rest):
                copies[l, r] = pltpu.make_async_copy(
                    mant.at[l, r, :, which], held.at[l, r], sems.at[l, r]
                )
                copies[l, r].start()
        spread = lax.broadcasted_iota(jnp.int32, (nblocks, columns), 1) // blocksize
        spread = spread == lax.broadcasted_iota(jnp.int32, (nblocks, columns), 0)
        spread = spread.astype(bf16)
        for l in range(local):
            for r in range(rest):
                copies[l, r].wait()
                for i in range(pair):
                    start = (((l * rest + r) * pair + i) * cores + which) * rows
                    power = exps[:, pl.ds(pl.multiple_of(start, 128), rows)].astype(f32)
                    factor = lax.dot_general(
                        jnp.exp2(power).astype(bf16),
                        spread,
                        (((0,), (0,)), ((), ())),
                        preferred_element_type=f32,
                    )
                    scaled = (held[l, r, i].astype(f32) * factor).astype(bf16)
                    for out, piece in zip(outs, pieces):
                        out[l, r // lead[2], r % lead[2], i] = scaled[piece]

    mant = values.reshape(local, rest, pair, cores, rows, columns)
    return pl.pallas_call(
        kernel,
        out_shape=[pltpu.VMEM(shape, bf16) for shape in shapes],
        in_specs=[
            pl.BlockSpec(memory_space=pltpu.VMEM),
            pl.BlockSpec(memory_space=pl.ANY),
        ],
        out_specs=[pl.BlockSpec(memory_space=pltpu.VMEM)] * parts,
        scratch_shapes=[
            pltpu.VMEM((local, rest, pair, rows, columns), bf16),
            pltpu.SemaphoreType.DMA((local, rest)),
        ],
        compiler_params=pltpu.CompilerParams(vmem_limit_bytes=16 * MIB),
        cost_estimate=pl.CostEstimate(flops=0, bytes_accessed=1, transcendentals=0),
        name="dequant",
    )(vmem(exponents), pltpu.with_memory_space_constraint(mant, pltpu.HBM))


class Unit:
    def __init__(self, grid, terms):
        self.grid, self.left = grid, "yvwx"
        self.terms = [(t, "yvwx") for t in terms]

    @staticmethod
    def entry(axes, where):
        return tuple(where.get(a, ALL) for a in axes)

    def hop(self, axis):
        grid, left = self.grid, self.left.replace(axis, "")
        arrays = [t for t, _ in self.terms]
        shape = tuple(grid.size[a] for a in left) + arrays[0].shape[-2:]

        def kernel(*refs):
            held, outs = refs[: len(arrays)], refs[len(arrays) :]
            place = grid.place()
            for d, out in zip(grid.others(axis), outs):
                where = {a: i for a, i in place.items() if a not in self.left}
                where[axis] = grid.step(axis, place[axis], d)
                parts = [t[self.entry(axes, where)] for t, (_, axes) in zip(held, self.terms)]
                out[...] = total(parts).astype(bf16)

        outs = [pltpu.VMEM(shape, bf16) for _ in grid.others(axis)]
        if outs:
            outs = call(kernel, "fold_" + axis, arrays, outs)
        self.left = left
        for d, out in zip(grid.others(axis), outs):
            self.terms.append((grid.send(out, **{axis: d}), left))


def project(grid, units, pieces, packs, rows, ranks, columns):
    size = grid.size
    each = ranks // grid.nodes
    arrays = [t for u in units for t, _ in u.terms]

    def kernel(*refs):
        held, refs = iter(refs[: len(arrays)]), refs[len(arrays) :]
        projs, refs = refs[: size["v"]], refs[size["v"] :]
        sends, outs, acc = refs[: size["v"]], refs[size["v"] : -1], refs[-1]
        place = grid.place()
        dims = (((0,), (0,)), ((), ()))
        for unit, piece in zip(units, pieces):
            terms = [(next(held), axes) for _, axes in unit.terms]
            for d, send in enumerate(sends):
                where = place | {"v": grid.step("v", place["v"], d)}
                value = total([t[Unit.entry(axes, where)] for t, axes in terms])
                send[piece] = value.astype(bf16)
        acc[...] = total(
            [
                lax.dot_general(came[:rows], send[...], dims, preferred_element_type=f32)
                for came, send in zip(projs, sends)
            ]
        )
        for d, out in enumerate(outs):
            there = {"c": grid.step("c", place["c"], d)}
            for e in range(size["x"]):
                there["x"] = grid.step("x", place["x"], e)
                for f in range(size["w"]):
                    there["w"] = grid.step("w", place["w"], f)
                    for v in range(size["v"]):
                        start = pl.multiple_of(grid.node(there | {"v": v}) * each, each)
                        out[e, f, v * each : (v + 1) * each] = acc[pl.ds(start, each)]

    out = call(
        kernel,
        "project",
        arrays + packs,
        [pltpu.VMEM((rows, columns), bf16)] * size["v"]
        + [pltpu.VMEM((size["x"], size["w"], size["v"] * each, columns), f32)] * size["c"],
        [pltpu.VMEM((ranks, columns), f32)],
        limit=12,
    )
    return out[: size["v"]], out[size["v"] :]


def add_cut(terms, name, run=1):
    count = terms[0].shape[0]

    def kernel(*refs):
        arrays, outs = refs[: len(terms)], refs[len(terms) :]
        for e, out in enumerate(outs):
            parts = [a[e] for a in arrays]
            runs = [total(parts[i : i + run]) for i in range(0, len(parts), run)]
            out[...] = total(runs).astype(out.dtype)

    return call(kernel, name, terms, [pltpu.VMEM(terms[0].shape[1:], bf16)] * count)


def add(terms, name, dtype):
    def kernel(*refs):
        *arrays, out = refs
        out[...] = total([a[...] for a in arrays]).astype(dtype)

    return call(kernel, name, terms, pltpu.VMEM(terms[0].shape, dtype))


def pack(proj, moments):
    rows, ranks = proj.shape
    each, columns = moments[0].shape
    cuts = columns // ranks

    def kernel(proj, moment1, moment2, out):
        out[:rows] = proj[...].astype(bf16)
        both = jnp.concatenate([moment1[...], moment2[...]], 0).astype(bf16)
        for h in range(cuts):
            start = rows + h * 2 * each
            out[start : start + 2 * each] = both[:, h * ranks : (h + 1) * ranks]

    shape = (rows + cuts * 2 * each, ranks)
    return call(kernel, "pack", [proj, *moments], pltpu.VMEM(shape, bf16))


def normalize(grid, parts, packs, rows, first, columns):
    ranks = packs[0].shape[1]
    group = parts[0].shape[1]
    each = ranks // grid.nodes
    cuts = columns // ranks
    rest = grid.size["v"]

    def kernel(*refs):
        v = grid.place()["v"]
        arrays, held = refs[: len(parts)], refs[len(parts) : len(parts) + rest]
        sums, mine, scratch = refs[len(parts) + rest :]
        scratch[...] = total([a[...] for a in arrays]).reshape(scratch.shape)
        mine[...] = scratch[v]
        raw, tilde = 0.0, 0.0
        for d in range(rest):
            value = scratch[grid.step("v", v, d)]
            old = []
            for h in range(cuts):
                start = rows + h * 2 * each
                old.append(held[d][start : start + 2 * each].astype(f32))
            old = jnp.concatenate(old, 1)[:, first : first + group]
            m1 = 0.9 * old[:each] + 0.1 * value
            m2 = 0.999 * old[each:] + 0.001 * value * value
            ratio = m1 / bias_first / (jnp.sqrt(m2 / bias_second) + 1e-08)
            raw += jnp.sum(value * value, 0, keepdims=True)
            tilde += jnp.sum(ratio * ratio, 0, keepdims=True)
        sums[...] = jnp.concatenate([raw, tilde, jnp.zeros((6, group), f32)], 0)

    return call(
        kernel,
        "normalize",
        parts + packs,
        [pltpu.VMEM((8, group), f32), pltpu.VMEM((each, group), f32)],
        [pltpu.VMEM((rest, each, group), f32)],
    )


def update(weights, moments, grads, sums, mine, blocksize):
    rows, columns = weights.shape

    def kernel(weights, moment1, moment2, *refs):
        grad_refs, refs = refs[: len(grads)], refs[len(grads) :]
        sum_refs, refs = refs[: len(sums)], refs[len(sums) :]
        mine, new_out, new1, new2, packed = refs
        packed[rows:, :] = jnp.zeros((PAD, columns), bf16)
        lane = lax.broadcasted_iota(jnp.int32, (rows, 128), 1)
        scales = jnp.zeros((rows, 128), f32)
        added = total([s[...] for s in sum_refs])
        col_scale = jnp.sqrt(added[1:2]) / jnp.sqrt(added[0:1] + 1e-06)
        for k in range(columns // blocksize):
            cols = slice(k * blocksize, (k + 1) * blocksize)
            grad = total([t[:, cols] for t in grad_refs])
            new = weights[:, cols] - 8.0 * grad * col_scale[:, cols]
            new_out[:, cols] = new
            scale = (jnp.max(jnp.abs(new), 1, keepdims=True) + 1e-06).astype(bf16).astype(f32)
            packed[:rows, cols] = (new / scale).astype(bf16)
            scales = jnp.where(lane == k, scale, scales)
        new1[...] = 0.9 * moment1[...] + 0.1 * mine[...]
        new2[...] = 0.999 * moment2[...] + 0.001 * mine[...] * mine[...]
        packed[rows:, :rows] = jnp.transpose(scales)[:PAD].astype(bf16)

    return call(
        kernel,
        "update",
        [weights, *moments, *grads, *sums, mine],
        [
            jax.ShapeDtypeStruct((rows, columns), f32),
            jax.ShapeDtypeStruct(moments[0].shape, f32),
            jax.ShapeDtypeStruct(moments[0].shape, f32),
            pltpu.VMEM((rows + PAD, columns), bf16),
        ],
    )


def lay(grid, held, nblocks, *begun):
    shards, steps = [t for t, _ in held], [step for _, step in held]
    rows, columns = shards[0].shape[0] - PAD, shards[0].shape[1]
    count = len(shards)

    def node_of(k):
        place = grid.place()
        return grid.node({a: grid.step(a, place[a], -steps[k][a]) for a in "vwxc"})

    if rows % 128:
        places = jnp.stack([node_of(k) for k in range(count)])
        order = jnp.zeros(count, jnp.int32).at[places].set(jnp.arange(count, dtype=jnp.int32))
        stacked = jnp.take(jnp.stack(shards), order, axis=0)
        values = stacked[:, :rows].reshape(count * rows, columns)
        scales = jnp.moveaxis(stacked[:, rows : rows + nblocks, :rows], 0, 1)
        return values, scales.reshape(nblocks, count * rows)

    def kernel(*refs):
        held, (values, scales, sems) = refs[:count], refs[count + len(begun) :]
        if begun:
            scales[...] = refs[count + 1][...]
        copies = []
        for k in range(count):
            start = pl.multiple_of(node_of(k) * rows, 128)
            copies.append(
                pltpu.make_async_copy(
                    held[k].at[pl.ds(0, rows)], values.at[pl.ds(start, rows)], sems.at[k]
                )
            )
            copies[-1].start()
        for k in range(count):
            start = pl.multiple_of(node_of(k) * rows, 128)
            tail = held[k][rows:, :rows].astype(f32)[:nblocks]
            scales[:, pl.ds(start, rows)] = tail.astype(bf16)
        for copy in copies:
            copy.wait()

    in_vmem, anywhere = (pl.BlockSpec(memory_space=m) for m in (pltpu.VMEM, pl.ANY))
    scales_shape = (nblocks, grid.nodes * rows)
    return pl.pallas_call(
        kernel,
        out_shape=[
            pltpu.HBM((grid.nodes * rows, columns), bf16),
            jax.ShapeDtypeStruct(scales_shape, bf16) if begun else pltpu.VMEM(scales_shape, bf16),
        ],
        in_specs=[in_vmem] * count + [anywhere, in_vmem][: len(begun)],
        out_specs=[anywhere, in_vmem],
        input_output_aliases={count: 0} if begun else {},
        scratch_shapes=[pltpu.SemaphoreType.DMA((count,))],
        compiler_params=pltpu.CompilerParams(vmem_limit_bytes=8 * MIB),
        cost_estimate=pl.CostEstimate(flops=0, bytes_accessed=1, transcendentals=0),
        name="lay",
    )(*[vmem(s) for s in shards], *begun)


def shards(grad_values, grad_exponents, proj, weights, moment1, moment2):
    grid = Grid()
    size = grid.size
    values, exponents = grad_values[0], grad_exponents[0]
    width, columns = values.shape
    nblocks = exponents.shape[0]
    blocksize = columns // nblocks
    rows = width // grid.nodes // size["y"]
    ranks = proj.shape[1]
    pieces = []
    for block, blocks, half, halves in PIECES:
        n, m = rows // halves, columns // blocks
        pieces.append((slice(half * n, (half + 1) * n), slice(block * m, (block + 1) * m)))

    other = dequant(grid, values, exponents, 1, rows, blocksize, pieces) if size["c"] > 1 else []
    other = [grid.send(t, c=1) for t in other]
    mine = dequant(grid, values, exponents, 0, rows, blocksize, pieces)
    units = [Unit(grid, list(terms)) for terms in zip(mine, *([other] if other else []))]
    for turn in range(3):
        for unit, order in zip(units, ORDERS):
            unit.hop(order[turn])

    packs = [pack(proj, [moment1, moment2])]
    packs += [grid.send(packs[0], v=-d) for d in grid.others("v")]

    parts, projected = project(grid, units, pieces, packs, rows, ranks, columns)
    received = [grid.send(t, v=d) for d, t in zip(grid.others("v"), parts[1:])]

    terms = [projected[0]] + [grid.send(projected[d], c=d) for d in grid.others("c")]
    by_x = add_cut(terms, "add_cores")
    by_y = []
    for dy in range(size["y"]):
        for dx in range(size["x"]):
            by_y.append(grid.send(by_x[dx], x=dx, y=dy) if dx or dy else by_x[0])
    if size["y"] > 2:
        stacked = jnp.stack(by_y).reshape((size["y"], -1) + by_y[0].shape)
        came = jnp.stack([grid.step("y", grid.place()["y"], -d) for d in range(size["y"])])
        order = jnp.zeros(size["y"], jnp.int32).at[came].set(jnp.arange(size["y"], dtype=jnp.int32))
        stacked = jnp.take(stacked, order, axis=0)
        by_y = [stacked[i, j] for i in range(size["y"]) for j in range(stacked.shape[1])]
    by_w = add_cut(by_y, "add_chips", size["x"])
    summed = [
        grid.send(by_w[dw], w=dw, v=dv) if dw or dv else by_w[0]
        for dv in range(size["v"])
        for dw in range(size["w"])
    ]
    added, kept = normalize(grid, summed, packs, rows, 0, columns)
    added = add([added] + [grid.send(added, c=d) for d in grid.others("c")], "add_sums", f32)
    sums = [
        grid.send(added, x=dx, w=dw) if dx or dw else added
        for dx in range(size["x"])
        for dw in range(size["w"])
    ]
    new, new1, new2, packed = update(
        weights, [moment1, moment2], [parts[0], *received], sums, kept, blocksize
    )

    along_v = [packed] + [grid.send(packed, v=d) for d in grid.others("v")]
    held = []
    for dv, over_v in enumerate(along_v):
        along_w = [over_v] + [grid.send(over_v, w=d) for d in grid.others("w")]
        for dw, over_w in enumerate(along_w):
            along_x = [over_w] + [grid.send(over_w, x=d) for d in grid.others("x")]
            for dx, over_x in enumerate(along_x):
                along_c = [over_x] + [grid.send(over_x, c=d) for d in grid.others("c")]
                for dc, shard in enumerate(along_c):
                    held.append((shard, {"v": dv, "w": dw, "x": dx, "c": dc}))
    late = [t for t in held if t[1]["v"] and t[1]["w"]]
    if late and rows % 128 == 0:
        early = [t for t in held if not (t[1]["v"] and t[1]["w"])]
        begun = lay(grid, early, nblocks)
        quant, scales = lay(grid, late, nblocks, *begun)
    else:
        quant, scales = lay(grid, held, nblocks)
    return quant, scales, new, new1, new2


def solution(mesh):
    return jax.shard_map(
        shards,
        mesh=mesh,
        in_specs=(
            P(("node", "local"), None, None),
            P(("node", "local"), None, None),
            P(("local", "node"), None),
            P(("local", "node"), None),
            P("node", None),
            P("node", None),
        ),
        out_specs=(
            P("local", None),
            P(None, "local"),
            P(("local", "node"), None),
            P("node", None),
            P("node", None),
        ),
        check_vma=False,
    )
```

```python
import functools

import jax
import jax.numpy as jnp
from jax import lax
from jax.experimental import pallas as pl
from jax.experimental.pallas import tpu as pltpu
from jax.sharding import PartitionSpec as P

f32, bf16 = jnp.float32, jnp.bfloat16
bias_first = 1.0 - 0.9**10
bias_second = 1.0 - 0.999**10
AXES = ("node", "local")
PIECES = ((0, 4, 0, 1), (1, 4, 0, 1), (2, 4, 0, 1), (3, 4, 0, 2), (3, 4, 1, 2))
ORDERS = ("xyw", "ywx", "wxy", "wyx", "yxw")
PAD = 16
ALL = slice(None)
MIB = 2**20


def total(terms):
    return functools.reduce(lambda a, b: a + b, [t.astype(f32) for t in terms])


def at(array, index, axis):
    return lax.dynamic_index_in_dim(array, index, axis, False)


def vmem(array):
    return pltpu.with_memory_space_constraint(array, pltpu.VMEM)


class Grid:
    def __init__(self):
        nodes, local = lax.axis_size("node"), lax.axis_size("local")
        size, left = {"y": local}, nodes
        for axis in "cxw":
            size[axis] = 2 if left % 2 == 0 else 1
            left //= size[axis]
        size["v"] = left
        self.size, self.nodes = size, nodes

    def split(self, node):
        place = {}
        for axis in "cxwv":
            place[axis], node = node % self.size[axis], node // self.size[axis]
        return place

    def node(self, place):
        node = 0
        for axis in "vwxc":
            node = node * self.size[axis] + place[axis]
        return node

    def place(self):
        place, node = {"y": lax.axis_index("local")}, lax.axis_index("node")
        for axis in "cxwv":
            place[axis] = lax.rem(node, self.size[axis])
            node = lax.div(node, self.size[axis])
        return place

    def step(self, axis, here, d):
        size = self.size[axis]
        if size & (size - 1):
            if isinstance(here, int):
                return (here + d) % size
            return lax.rem(here + (d + size) % size, size)
        if isinstance(here, int):
            return here ^ abs(d)
        return lax.bitwise_xor(here, jnp.int32(abs(d)))

    def others(self, axis):
        return range(1, self.size[axis])

    def send(self, array, **steps):
        local, pairs = self.size["y"], []
        for n in range(self.nodes):
            for y in range(local):
                place = self.split(n) | {"y": y}
                there = {a: self.step(a, i, steps.get(a, 0)) for a, i in place.items()}
                pairs.append((n * local + y, self.node(there) * local + there["y"]))
        return lax.ppermute(array, AXES, pairs)


def call(kernel, name, arrays, outs, scratch=(), limit=8):
    return pl.pallas_call(
        kernel,
        out_shape=outs,
        in_specs=[pl.BlockSpec(memory_space=pltpu.VMEM)] * len(arrays),
        out_specs=jax.tree.map(lambda _: pl.BlockSpec(memory_space=pltpu.VMEM), outs),
        scratch_shapes=scratch,
        compiler_params=pltpu.CompilerParams(vmem_limit_bytes=limit * MIB),
        cost_estimate=pl.CostEstimate(flops=0, bytes_accessed=1, transcendentals=0),
        name=name,
    )(*[vmem(a) for a in arrays])


def dequant(grid, values, exponents, away, rows, blocksize, pieces):
    cores, local, pair = (grid.size[a] for a in "cyx")
    rest = grid.size["v"] * grid.size["w"]
    lead, parts = tuple(grid.size[a] for a in "yvwx"), len(pieces)
    shapes = [lead + (p[0].stop - p[0].start, p[1].stop - p[1].start) for p in pieces]
    nblocks, columns = exponents.shape[0], values.shape[1]
    if rows % 128:
        which = grid.step("c", grid.place()["c"], away)
        power = jnp.exp2(exponents.astype(f32)).astype(bf16)
        picked = power.reshape(-1, local, rest, pair, cores, rows)
        picked = jnp.moveaxis(at(picked, which, 4), 0, -1)
        mant = at(values.reshape(local, rest, pair, cores, rows, -1, blocksize), which, 3)
        out = (mant * picked[..., None]).reshape(lead + (rows, columns))
        return [out[(..., *p)] for p in pieces]

    def kernel(exps, mant, *refs):
        outs, (held, sems) = refs[:parts], refs[parts:]
        which = grid.step("c", grid.place()["c"], away)
        copies = {}
        for l in range(local):
            for r in range(rest):
                copies[l, r] = pltpu.make_async_copy(
                    mant.at[l, r, :, which], held.at[l, r], sems.at[l, r]
                )
                copies[l, r].start()
        spread = lax.broadcasted_iota(jnp.int32, (nblocks, columns), 1) // blocksize
        spread = spread == lax.broadcasted_iota(jnp.int32, (nblocks, columns), 0)
        spread = spread.astype(bf16)
        for l in range(local):
            for r in range(rest):
                copies[l, r].wait()
                for i in range(pair):
                    start = (((l * rest + r) * pair + i) * cores + which) * rows
                    power = exps[:, pl.ds(pl.multiple_of(start, 128), rows)].astype(f32)
                    factor = lax.dot_general(
                        jnp.exp2(power).astype(bf16),
                        spread,
                        (((0,), (0,)), ((), ())),
                        preferred_element_type=f32,
                    )
                    scaled = (held[l, r, i].astype(f32) * factor).astype(bf16)
                    for out, piece in zip(outs, pieces):
                        out[l, r // lead[2], r % lead[2], i] = scaled[piece]

    mant = values.reshape(local, rest, pair, cores, rows, columns)
    return pl.pallas_call(
        kernel,
        out_shape=[pltpu.VMEM(shape, bf16) for shape in shapes],
        in_specs=[
            pl.BlockSpec(memory_space=pltpu.VMEM),
            pl.BlockSpec(memory_space=pl.ANY),
        ],
        out_specs=[pl.BlockSpec(memory_space=pltpu.VMEM)] * parts,
        scratch_shapes=[
            pltpu.VMEM((local, rest, pair, rows, columns), bf16),
            pltpu.SemaphoreType.DMA((local, rest)),
        ],
        compiler_params=pltpu.CompilerParams(vmem_limit_bytes=16 * MIB),
        cost_estimate=pl.CostEstimate(flops=0, bytes_accessed=1, transcendentals=0),
        name="dequant",
    )(vmem(exponents), pltpu.with_memory_space_constraint(mant, pltpu.HBM))


class Unit:
    def __init__(self, grid, terms):
        self.grid, self.left = grid, "yvwx"
        self.terms = [(t, "yvwx") for t in terms]

    @staticmethod
    def entry(axes, where):
        return tuple(where.get(a, ALL) for a in axes)

    def hop(self, axis):
        grid, left = self.grid, self.left.replace(axis, "")
        arrays = [t for t, _ in self.terms]
        shape = tuple(grid.size[a] for a in left) + arrays[0].shape[-2:]

        def kernel(*refs):
            held, outs = refs[: len(arrays)], refs[len(arrays) :]
            place = grid.place()
            for d, out in zip(grid.others(axis), outs):
                where = {a: i for a, i in place.items() if a not in self.left}
                where[axis] = grid.step(axis, place[axis], d)
                parts = [t[self.entry(axes, where)] for t, (_, axes) in zip(held, self.terms)]
                out[...] = total(parts).astype(bf16)

        outs = [pltpu.VMEM(shape, bf16) for _ in grid.others(axis)]
        if outs:
            outs = call(kernel, "fold_" + axis, arrays, outs)
        self.left = left
        for d, out in zip(grid.others(axis), outs):
            self.terms.append((grid.send(out, **{axis: d}), left))


def project(grid, units, pieces, packs, rows, ranks, columns):
    size = grid.size
    each = ranks // grid.nodes
    arrays = [t for u in units for t, _ in u.terms]

    def kernel(*refs):
        held, refs = iter(refs[: len(arrays)]), refs[len(arrays) :]
        projs, refs = refs[: size["v"]], refs[size["v"] :]
        sends, outs, acc = refs[: size["v"]], refs[size["v"] : -1], refs[-1]
        place = grid.place()
        dims = (((0,), (0,)), ((), ()))
        for unit, piece in zip(units, pieces):
            terms = [(next(held), axes) for _, axes in unit.terms]
            for d, send in enumerate(sends):
                where = place | {"v": grid.step("v", place["v"], d)}
                value = total([t[Unit.entry(axes, where)] for t, axes in terms])
                send[piece] = value.astype(bf16)
        acc[...] = total(
            [
                lax.dot_general(came[:rows], send[...], dims, preferred_element_type=f32)
                for came, send in zip(projs, sends)
            ]
        )
        for d, out in enumerate(outs):
            there = {"c": grid.step("c", place["c"], d)}
            for e in range(size["x"]):
                there["x"] = grid.step("x", place["x"], e)
                for f in range(size["w"]):
                    there["w"] = grid.step("w", place["w"], f)
                    for v in range(size["v"]):
                        start = pl.multiple_of(grid.node(there | {"v": v}) * each, each)
                        out[e, f, v * each : (v + 1) * each] = acc[pl.ds(start, each)]

    out = call(
        kernel,
        "project",
        arrays + packs,
        [pltpu.VMEM((rows, columns), bf16)] * size["v"]
        + [pltpu.VMEM((size["x"], size["w"], size["v"] * each, columns), f32)] * size["c"],
        [pltpu.VMEM((ranks, columns), f32)],
        limit=12,
    )
    return out[: size["v"]], out[size["v"] :]


def add_cut(terms, name, run=1):
    count = terms[0].shape[0]

    def kernel(*refs):
        arrays, outs = refs[: len(terms)], refs[len(terms) :]
        for e, out in enumerate(outs):
            parts = [a[e] for a in arrays]
            runs = [total(parts[i : i + run]) for i in range(0, len(parts), run)]
            out[...] = total(runs).astype(out.dtype)

    return call(kernel, name, terms, [pltpu.VMEM(terms[0].shape[1:], bf16)] * count)


def add(terms, name, dtype):
    def kernel(*refs):
        *arrays, out = refs
        out[...] = total([a[...] for a in arrays]).astype(dtype)

    return call(kernel, name, terms, pltpu.VMEM(terms[0].shape, dtype))


def pack(proj, moments):
    rows, ranks = proj.shape
    each, columns = moments[0].shape
    cuts = columns // ranks

    def kernel(proj, moment1, moment2, out):
        out[:rows] = proj[...].astype(bf16)
        both = jnp.concatenate([moment1[...], moment2[...]], 0).astype(bf16)
        for h in range(cuts):
            start = rows + h * 2 * each
            out[start : start + 2 * each] = both[:, h * ranks : (h + 1) * ranks]

    shape = (rows + cuts * 2 * each, ranks)
    return call(kernel, "pack", [proj, *moments], pltpu.VMEM(shape, bf16))


def normalize(grid, parts, packs, rows, first, columns):
    ranks = packs[0].shape[1]
    group = parts[0].shape[1]
    each = ranks // grid.nodes
    cuts = columns // ranks
    rest = grid.size["v"]

    def kernel(*refs):
        v = grid.place()["v"]
        arrays, held = refs[: len(parts)], refs[len(parts) : len(parts) + rest]
        sums, mine, scratch = refs[len(parts) + rest :]
        scratch[...] = total([a[...] for a in arrays]).reshape(scratch.shape)
        mine[...] = scratch[v]
        raw, tilde = 0.0, 0.0
        for d in range(rest):
            value = scratch[grid.step("v", v, d)]
            old = []
            for h in range(cuts):
                start = rows + h * 2 * each
                old.append(held[d][start : start + 2 * each].astype(f32))
            old = jnp.concatenate(old, 1)[:, first : first + group]
            m1 = 0.9 * old[:each] + 0.1 * value
            m2 = 0.999 * old[each:] + 0.001 * value * value
            ratio = m1 / bias_first / (jnp.sqrt(m2 / bias_second) + 1e-08)
            raw += jnp.sum(value * value, 0, keepdims=True)
            tilde += jnp.sum(ratio * ratio, 0, keepdims=True)
        sums[...] = jnp.concatenate([raw, tilde, jnp.zeros((6, group), f32)], 0)

    return call(
        kernel,
        "normalize",
        parts + packs,
        [pltpu.VMEM((8, group), f32), pltpu.VMEM((each, group), f32)],
        [pltpu.VMEM((rest, each, group), f32)],
    )


def update(weights, moments, grads, sums, mine, blocksize):
    rows, columns = weights.shape

    def kernel(weights, moment1, moment2, *refs):
        grad_refs, refs = refs[: len(grads)], refs[len(grads) :]
        sum_refs, refs = refs[: len(sums)], refs[len(sums) :]
        mine, new_out, new1, new2, packed = refs
        packed[rows:, :] = jnp.zeros((PAD, columns), bf16)
        lane = lax.broadcasted_iota(jnp.int32, (rows, 128), 1)
        scales = jnp.zeros((rows, 128), f32)
        added = total([s[...] for s in sum_refs])
        col_scale = jnp.sqrt(added[1:2]) / jnp.sqrt(added[0:1] + 1e-06)
        for k in range(columns // blocksize):
            cols = slice(k * blocksize, (k + 1) * blocksize)
            grad = total([t[:, cols] for t in grad_refs])
            new = weights[:, cols] - 8.0 * grad * col_scale[:, cols]
            new_out[:, cols] = new
            scale = (jnp.max(jnp.abs(new), 1, keepdims=True) + 1e-06).astype(bf16).astype(f32)
            packed[:rows, cols] = (new / scale).astype(bf16)
            scales = jnp.where(lane == k, scale, scales)
        new1[...] = 0.9 * moment1[...] + 0.1 * mine[...]
        new2[...] = 0.999 * moment2[...] + 0.001 * mine[...] * mine[...]
        packed[rows:, :rows] = jnp.transpose(scales)[:PAD].astype(bf16)

    return call(
        kernel,
        "update",
        [weights, *moments, *grads, *sums, mine],
        [
            jax.ShapeDtypeStruct((rows, columns), f32),
            jax.ShapeDtypeStruct(moments[0].shape, f32),
            jax.ShapeDtypeStruct(moments[0].shape, f32),
            pltpu.VMEM((rows + PAD, columns), bf16),
        ],
    )


def lay(grid, held, nblocks, *begun):
    shards, steps = [t for t, _ in held], [step for _, step in held]
    rows, columns = shards[0].shape[0] - PAD, shards[0].shape[1]
    count = len(shards)

    def node_of(k):
        place = grid.place()
        return grid.node({a: grid.step(a, place[a], -steps[k][a]) for a in "vwxc"})

    if rows % 128:
        places = jnp.stack([node_of(k) for k in range(count)])
        order = jnp.zeros(count, jnp.int32).at[places].set(jnp.arange(count, dtype=jnp.int32))
        stacked = jnp.take(jnp.stack(shards), order, axis=0)
        values = stacked[:, :rows].reshape(count * rows, columns)
        scales = jnp.moveaxis(stacked[:, rows : rows + nblocks, :rows], 0, 1)
        return values, scales.reshape(nblocks, count * rows)

    def kernel(*refs):
        held, (values, scales, sems) = refs[:count], refs[count + len(begun) :]
        if begun:
            scales[...] = refs[count + 1][...]
        copies = []
        for k in range(count):
            start = pl.multiple_of(node_of(k) * rows, 128)
            copies.append(
                pltpu.make_async_copy(
                    held[k].at[pl.ds(0, rows)], values.at[pl.ds(start, rows)], sems.at[k]
                )
            )
            copies[-1].start()
        for k in range(count):
            start = pl.multiple_of(node_of(k) * rows, 128)
            tail = held[k][rows:, :rows].astype(f32)[:nblocks]
            scales[:, pl.ds(start, rows)] = tail.astype(bf16)
        for copy in copies:
            copy.wait()

    in_vmem, anywhere = (pl.BlockSpec(memory_space=m) for m in (pltpu.VMEM, pl.ANY))
    scales_shape = (nblocks, grid.nodes * rows)
    return pl.pallas_call(
        kernel,
        out_shape=[
            pltpu.HBM((grid.nodes * rows, columns), bf16),
            jax.ShapeDtypeStruct(scales_shape, bf16) if begun else pltpu.VMEM(scales_shape, bf16),
        ],
        in_specs=[in_vmem] * count + [anywhere, in_vmem][: len(begun)],
        out_specs=[anywhere, in_vmem],
        input_output_aliases={count: 0} if begun else {},
        scratch_shapes=[pltpu.SemaphoreType.DMA((count,))],
        compiler_params=pltpu.CompilerParams(vmem_limit_bytes=8 * MIB),
        cost_estimate=pl.CostEstimate(flops=0, bytes_accessed=1, transcendentals=0),
        name="lay",
    )(*[vmem(s) for s in shards], *begun)


def shards(grad_values, grad_exponents, proj, weights, moment1, moment2):
    grid = Grid()
    size = grid.size
    values, exponents = grad_values[0], grad_exponents[0]
    width, columns = values.shape
    nblocks = exponents.shape[0]
    blocksize = columns // nblocks
    rows = width // grid.nodes // size["y"]
    ranks = proj.shape[1]
    pieces = []
    for block, blocks, half, halves in PIECES:
        n, m = rows // halves, columns // blocks
        pieces.append((slice(half * n, (half + 1) * n), slice(block * m, (block + 1) * m)))

    other = dequant(grid, values, exponents, 1, rows, blocksize, pieces) if size["c"] > 1 else []
    other = [grid.send(t, c=1) for t in other]
    mine = dequant(grid, values, exponents, 0, rows, blocksize, pieces)
    units = [Unit(grid, list(terms)) for terms in zip(mine, *([other] if other else []))]
    for turn in range(3):
        for unit, order in zip(units, ORDERS):
            unit.hop(order[turn])

    packs = [pack(proj, [moment1, moment2])]
    packs += [grid.send(packs[0], v=-d) for d in grid.others("v")]

    parts, projected = project(grid, units, pieces, packs, rows, ranks, columns)
    received = [grid.send(t, v=d) for d, t in zip(grid.others("v"), parts[1:])]

    terms = [projected[0]] + [grid.send(projected[d], c=d) for d in grid.others("c")]
    by_x = add_cut(terms, "add_cores")
    by_y = []
    for dy in range(size["y"]):
        for dx in range(size["x"]):
            by_y.append(grid.send(by_x[dx], x=dx, y=dy) if dx or dy else by_x[0])
    if size["y"] > 2:
        stacked = jnp.stack(by_y).reshape((size["y"], -1) + by_y[0].shape)
        came = jnp.stack([grid.step("y", grid.place()["y"], -d) for d in range(size["y"])])
        order = jnp.zeros(size["y"], jnp.int32).at[came].set(jnp.arange(size["y"], dtype=jnp.int32))
        stacked = jnp.take(stacked, order, axis=0)
        by_y = [stacked[i, j] for i in range(size["y"]) for j in range(stacked.shape[1])]
    by_w = add_cut(by_y, "add_chips", size["x"])
    summed = [
        grid.send(by_w[dw], w=dw, v=dv) if dw or dv else by_w[0]
        for dv in range(size["v"])
        for dw in range(size["w"])
    ]
    added, kept = normalize(grid, summed, packs, rows, 0, columns)
    added = add([added] + [grid.send(added, c=d) for d in grid.others("c")], "add_sums", f32)
    sums = [
        grid.send(added, x=dx, w=dw) if dx or dw else added
        for dx in range(size["x"])
        for dw in range(size["w"])
    ]
    new, new1, new2, packed = update(
        weights, [moment1, moment2], [parts[0], *received], sums, kept, blocksize
    )

    along_v = [packed] + [grid.send(packed, v=d) for d in grid.others("v")]
    held = []
    for dv, over_v in enumerate(along_v):
        along_w = [over_v] + [grid.send(over_v, w=d) for d in grid.others("w")]
        for dw, over_w in enumerate(along_w):
            along_x = [over_w] + [grid.send(over_w, x=d) for d in grid.others("x")]
            for dx, over_x in enumerate(along_x):
                along_c = [over_x] + [grid.send(over_x, c=d) for d in grid.others("c")]
                for dc, shard in enumerate(along_c):
                    held.append((shard, {"v": dv, "w": dw, "x": dx, "c": dc}))
    late = [t for t in held if t[1]["v"] and t[1]["w"]]
    if late and rows % 128 == 0:
        early = [t for t in held if not (t[1]["v"] and t[1]["w"])]
        begun = lay(grid, early, nblocks)
        quant, scales = lay(grid, late, nblocks, *begun)
    else:
        quant, scales = lay(grid, held, nblocks)
    return quant, scales, new, new1, new2


def solution(mesh):
    return jax.shard_map(
        shards,
        mesh=mesh,
        in_specs=(
            P(("node", "local"), None, None),
            P(("node", "local"), None, None),
            P(("local", "node"), None),
            P(("local", "node"), None),
            P("node", None),
            P("node", None),
        ),
        out_specs=(
            P("local", None),
            P(None, "local"),
            P(("local", "node"), None),
            P("node", None),
            P("node", None),
        ),
        check_vma=False,
    )
```

```python
import functools

import jax
import jax.numpy as jnp
from jax import lax
from jax.experimental import pallas as pl
from jax.experimental.pallas import tpu as pltpu
from jax.sharding import PartitionSpec as P

f32, bf16 = jnp.float32, jnp.bfloat16
bias_first = 1.0 - 0.9**10
bias_second = 1.0 - 0.999**10
AXES = ("node", "local")
PIECES = ((0, 4, 0, 1), (1, 4, 0, 1), (2, 4, 0, 1), (3, 4, 0, 2), (3, 4, 1, 2))
ORDERS = ("xyw", "ywx", "wxy", "wyx", "yxw")
PAD = 8
ALL = slice(None)
MIB = 2**20


def total(terms):
    return functools.reduce(lambda a, b: a + b, [t.astype(f32) for t in terms])


def at(array, index, axis):
    return lax.dynamic_index_in_dim(array, index, axis, False)


def vmem(array):
    return pltpu.with_memory_space_constraint(array, pltpu.VMEM)


class Grid:
    def __init__(self):
        nodes, local = lax.axis_size("node"), lax.axis_size("local")
        size, left = {"y": local}, nodes
        for axis in "cxw":
            size[axis] = 2 if left % 2 == 0 else 1
            left //= size[axis]
        size["v"] = left
        self.size, self.nodes = size, nodes

    def split(self, node):
        place = {}
        for axis in "cxwv":
            place[axis], node = node % self.size[axis], node // self.size[axis]
        return place

    def node(self, place):
        node = 0
        for axis in "vwxc":
            node = node * self.size[axis] + place[axis]
        return node

    def place(self):
        place, node = {"y": lax.axis_index("local")}, lax.axis_index("node")
        for axis in "cxwv":
            place[axis] = lax.rem(node, self.size[axis])
            node = lax.div(node, self.size[axis])
        return place

    def step(self, axis, here, d):
        size = self.size[axis]
        if size & (size - 1):
            if isinstance(here, int):
                return (here + d) % size
            return lax.rem(here + (d + size) % size, size)
        if isinstance(here, int):
            return here ^ abs(d)
        return lax.bitwise_xor(here, jnp.int32(abs(d)))

    def others(self, axis):
        return range(1, self.size[axis])

    def send(self, array, **steps):
        local, pairs = self.size["y"], []
        for n in range(self.nodes):
            for y in range(local):
                place = self.split(n) | {"y": y}
                there = {a: self.step(a, i, steps.get(a, 0)) for a, i in place.items()}
                pairs.append((n * local + y, self.node(there) * local + there["y"]))
        return lax.ppermute(array, AXES, pairs)


def call(kernel, name, arrays, outs, scratch=(), limit=8):
    return pl.pallas_call(
        kernel,
        out_shape=outs,
        in_specs=[pl.BlockSpec(memory_space=pltpu.VMEM)] * len(arrays),
        out_specs=jax.tree.map(lambda _: pl.BlockSpec(memory_space=pltpu.VMEM), outs),
        scratch_shapes=scratch,
        compiler_params=pltpu.CompilerParams(vmem_limit_bytes=limit * MIB),
        cost_estimate=pl.CostEstimate(flops=0, bytes_accessed=1, transcendentals=0),
        name=name,
    )(*[vmem(a) for a in arrays])


def dequant(grid, values, exponents, away, rows, blocksize, pieces):
    cores, local, pair = (grid.size[a] for a in "cyx")
    rest = grid.size["v"] * grid.size["w"]
    lead, parts = tuple(grid.size[a] for a in "yvwx"), len(pieces)
    shapes = [lead + (p[0].stop - p[0].start, p[1].stop - p[1].start) for p in pieces]
    nblocks, columns = exponents.shape[0], values.shape[1]
    if rows % 128:
        which = grid.step("c", grid.place()["c"], away)
        power = jnp.exp2(exponents.astype(f32)).astype(bf16)
        picked = power.reshape(-1, local, rest, pair, cores, rows)
        picked = jnp.moveaxis(at(picked, which, 4), 0, -1)
        mant = at(values.reshape(local, rest, pair, cores, rows, -1, blocksize), which, 3)
        out = (mant * picked[..., None]).reshape(lead + (rows, columns))
        return [out[(..., *p)] for p in pieces]

    def kernel(exps, mant, *refs):
        outs, (held, sems) = refs[:parts], refs[parts:]
        which = grid.step("c", grid.place()["c"], away)
        copies = {}
        for l in range(local):
            for r in range(rest):
                copies[l, r] = pltpu.make_async_copy(
                    mant.at[l, r, :, which], held.at[l, r], sems.at[l, r]
                )
                copies[l, r].start()
        spread = lax.broadcasted_iota(jnp.int32, (nblocks, columns), 1) // blocksize
        spread = spread == lax.broadcasted_iota(jnp.int32, (nblocks, columns), 0)
        spread = spread.astype(bf16)
        for l in range(local):
            for r in range(rest):
                copies[l, r].wait()
                for i in range(pair):
                    start = (((l * rest + r) * pair + i) * cores + which) * rows
                    power = exps[:, pl.ds(pl.multiple_of(start, 128), rows)].astype(f32)
                    factor = lax.dot_general(
                        jnp.exp2(power).astype(bf16),
                        spread,
                        (((0,), (0,)), ((), ())),
                        preferred_element_type=f32,
                    )
                    scaled = (held[l, r, i].astype(f32) * factor).astype(bf16)
                    for out, piece in zip(outs, pieces):
                        out[l, r // lead[2], r % lead[2], i] = scaled[piece]

    mant = values.reshape(local, rest, pair, cores, rows, columns)
    return pl.pallas_call(
        kernel,
        out_shape=[pltpu.VMEM(shape, bf16) for shape in shapes],
        in_specs=[
            pl.BlockSpec(memory_space=pltpu.VMEM),
            pl.BlockSpec(memory_space=pl.ANY),
        ],
        out_specs=[pl.BlockSpec(memory_space=pltpu.VMEM)] * parts,
        scratch_shapes=[
            pltpu.VMEM((local, rest, pair, rows, columns), bf16),
            pltpu.SemaphoreType.DMA((local, rest)),
        ],
        compiler_params=pltpu.CompilerParams(vmem_limit_bytes=16 * MIB),
        cost_estimate=pl.CostEstimate(flops=0, bytes_accessed=1, transcendentals=0),
        name="dequant",
    )(vmem(exponents), pltpu.with_memory_space_constraint(mant, pltpu.HBM))


class Unit:
    def __init__(self, grid, terms):
        self.grid, self.left = grid, "yvwx"
        self.terms = [(t, "yvwx") for t in terms]

    @staticmethod
    def entry(axes, where):
        return tuple(where.get(a, ALL) for a in axes)

    def hop(self, axis):
        grid, left = self.grid, self.left.replace(axis, "")
        arrays = [t for t, _ in self.terms]
        shape = tuple(grid.size[a] for a in left) + arrays[0].shape[-2:]

        def kernel(*refs):
            held, outs = refs[: len(arrays)], refs[len(arrays) :]
            place = grid.place()
            for d, out in zip(grid.others(axis), outs):
                where = {a: i for a, i in place.items() if a not in self.left}
                where[axis] = grid.step(axis, place[axis], d)
                parts = [t[self.entry(axes, where)] for t, (_, axes) in zip(held, self.terms)]
                out[...] = total(parts).astype(bf16)

        outs = [pltpu.VMEM(shape, bf16) for _ in grid.others(axis)]
        if outs:
            outs = call(kernel, "fold_" + axis, arrays, outs)
        self.left = left
        for d, out in zip(grid.others(axis), outs):
            self.terms.append((grid.send(out, **{axis: d}), left))


def project(grid, units, pieces, packs, rows, ranks, columns):
    size = grid.size
    each = ranks // grid.nodes
    arrays = [t for u in units for t, _ in u.terms]

    def kernel(*refs):
        held, refs = iter(refs[: len(arrays)]), refs[len(arrays) :]
        projs, refs = refs[: size["v"]], refs[size["v"] :]
        sends, outs, acc = refs[: size["v"]], refs[size["v"] : -1], refs[-1]
        place = grid.place()
        dims = (((0,), (0,)), ((), ()))
        for unit, piece in zip(units, pieces):
            terms = [(next(held), axes) for _, axes in unit.terms]
            for d, send in enumerate(sends):
                where = place | {"v": grid.step("v", place["v"], d)}
                value = total([t[Unit.entry(axes, where)] for t, axes in terms])
                send[piece] = value.astype(bf16)
        acc[...] = total(
            [
                lax.dot_general(came[:rows], send[...], dims, preferred_element_type=f32)
                for came, send in zip(projs, sends)
            ]
        )
        for d, out in enumerate(outs):
            there = {"c": grid.step("c", place["c"], d)}
            for e in range(size["x"]):
                there["x"] = grid.step("x", place["x"], e)
                for f in range(size["w"]):
                    there["w"] = grid.step("w", place["w"], f)
                    for v in range(size["v"]):
                        start = pl.multiple_of(grid.node(there | {"v": v}) * each, each)
                        out[e, f, v * each : (v + 1) * each] = acc[pl.ds(start, each)]

    out = call(
        kernel,
        "project",
        arrays + packs,
        [pltpu.VMEM((rows, columns), bf16)] * size["v"]
        + [pltpu.VMEM((size["x"], size["w"], size["v"] * each, columns), f32)] * size["c"],
        [pltpu.VMEM((ranks, columns), f32)],
        limit=12,
    )
    return out[: size["v"]], out[size["v"] :]


def add_cut(terms, name, run=1):
    count = terms[0].shape[0]

    def kernel(*refs):
        arrays, outs = refs[: len(terms)], refs[len(terms) :]
        for e, out in enumerate(outs):
            parts = [a[e] for a in arrays]
            runs = [total(parts[i : i + run]) for i in range(0, len(parts), run)]
            out[...] = total(runs).astype(out.dtype)

    return call(kernel, name, terms, [pltpu.VMEM(terms[0].shape[1:], bf16)] * count)


def add(terms, name, dtype):
    def kernel(*refs):
        *arrays, out = refs
        out[...] = total([a[...] for a in arrays]).astype(dtype)

    return call(kernel, name, terms, pltpu.VMEM(terms[0].shape, dtype))


def pack(proj, moments):
    rows, ranks = proj.shape
    each, columns = moments[0].shape
    cuts = columns // ranks

    def kernel(proj, moment1, moment2, out):
        out[:rows] = proj[...].astype(bf16)
        both = jnp.concatenate([moment1[...], moment2[...]], 0).astype(bf16)
        for h in range(cuts):
            start = rows + h * 2 * each
            out[start : start + 2 * each] = both[:, h * ranks : (h + 1) * ranks]

    shape = (rows + cuts * 2 * each, ranks)
    return call(kernel, "pack", [proj, *moments], pltpu.VMEM(shape, bf16))


def normalize(grid, parts, packs, rows, first, columns):
    ranks = packs[0].shape[1]
    group = parts[0].shape[1]
    each = ranks // grid.nodes
    cuts = columns // ranks
    rest = grid.size["v"]

    def kernel(*refs):
        v = grid.place()["v"]
        arrays, held = refs[: len(parts)], refs[len(parts) : len(parts) + rest]
        sums, mine, scratch = refs[len(parts) + rest :]
        scratch[...] = total([a[...] for a in arrays]).reshape(scratch.shape)
        mine[...] = scratch[v]
        raw, tilde = 0.0, 0.0
        for d in range(rest):
            value = scratch[grid.step("v", v, d)]
            old = []
            for h in range(cuts):
                start = rows + h * 2 * each
                old.append(held[d][start : start + 2 * each].astype(f32))
            old = jnp.concatenate(old, 1)[:, first : first + group]
            m1 = 0.9 * old[:each] + 0.1 * value
            m2 = 0.999 * old[each:] + 0.001 * value * value
            ratio = m1 / bias_first / (jnp.sqrt(m2 / bias_second) + 1e-08)
            raw += jnp.sum(value * value, 0, keepdims=True)
            tilde += jnp.sum(ratio * ratio, 0, keepdims=True)
        sums[...] = jnp.concatenate([raw, tilde, jnp.zeros((6, group), f32)], 0)

    return call(
        kernel,
        "normalize",
        parts + packs,
        [pltpu.VMEM((8, group), f32), pltpu.VMEM((each, group), f32)],
        [pltpu.VMEM((rest, each, group), f32)],
    )


def update(weights, moments, grads, sums, mine, blocksize):
    rows, columns = weights.shape

    def kernel(weights, moment1, moment2, *refs):
        grad_refs, refs = refs[: len(grads)], refs[len(grads) :]
        sum_refs, refs = refs[: len(sums)], refs[len(sums) :]
        mine, new_out, new1, new2, packed = refs
        packed[rows:, :] = jnp.zeros((PAD, columns), bf16)
        lane = lax.broadcasted_iota(jnp.int32, (rows, 128), 1)
        scales = jnp.zeros((rows, 128), f32)
        added = total([s[...] for s in sum_refs])
        col_scale = jnp.sqrt(added[1:2]) / jnp.sqrt(added[0:1] + 1e-06)
        for k in range(columns // blocksize):
            cols = slice(k * blocksize, (k + 1) * blocksize)
            grad = total([t[:, cols] for t in grad_refs])
            new = weights[:, cols] - 8.0 * grad * col_scale[:, cols]
            new_out[:, cols] = new
            scale = (jnp.max(jnp.abs(new), 1, keepdims=True) + 1e-06).astype(bf16).astype(f32)
            packed[:rows, cols] = (new / scale).astype(bf16)
            scales = jnp.where(lane == k, scale, scales)
        new1[...] = 0.9 * moment1[...] + 0.1 * mine[...]
        new2[...] = 0.999 * moment2[...] + 0.001 * mine[...] * mine[...]
        packed[rows:, :rows] = jnp.transpose(scales)[:PAD].astype(bf16)

    return call(
        kernel,
        "update",
        [weights, *moments, *grads, *sums, mine],
        [
            jax.ShapeDtypeStruct((rows, columns), f32),
            jax.ShapeDtypeStruct(moments[0].shape, f32),
            jax.ShapeDtypeStruct(moments[0].shape, f32),
            pltpu.VMEM((rows + PAD, columns), bf16),
        ],
    )


def lay(grid, held, nblocks, *begun):
    shards, steps = [t for t, _ in held], [step for _, step in held]
    rows, columns = shards[0].shape[0] - PAD, shards[0].shape[1]
    count = len(shards)

    def node_of(k):
        place = grid.place()
        return grid.node({a: grid.step(a, place[a], -steps[k][a]) for a in "vwxc"})

    if rows % 128:
        places = jnp.stack([node_of(k) for k in range(count)])
        order = jnp.zeros(count, jnp.int32).at[places].set(jnp.arange(count, dtype=jnp.int32))
        stacked = jnp.take(jnp.stack(shards), order, axis=0)
        values = stacked[:, :rows].reshape(count * rows, columns)
        scales = jnp.moveaxis(stacked[:, rows : rows + nblocks, :rows], 0, 1)
        return values, scales.reshape(nblocks, count * rows)

    def kernel(*refs):
        held, (values, scales, sems) = refs[:count], refs[count + len(begun) :]
        if begun:
            scales[...] = refs[count + 1][...]
        copies = []
        for k in range(count):
            start = pl.multiple_of(node_of(k) * rows, 128)
            copies.append(
                pltpu.make_async_copy(
                    held[k].at[pl.ds(0, rows)], values.at[pl.ds(start, rows)], sems.at[k]
                )
            )
            copies[-1].start()
        for k in range(count):
            start = pl.multiple_of(node_of(k) * rows, 128)
            tail = held[k][rows:, :rows].astype(f32)[:nblocks]
            scales[:, pl.ds(start, rows)] = tail.astype(bf16)
        for copy in copies:
            copy.wait()

    in_vmem, anywhere = (pl.BlockSpec(memory_space=m) for m in (pltpu.VMEM, pl.ANY))
    scales_shape = (nblocks, grid.nodes * rows)
    return pl.pallas_call(
        kernel,
        out_shape=[
            pltpu.HBM((grid.nodes * rows, columns), bf16),
            jax.ShapeDtypeStruct(scales_shape, bf16) if begun else pltpu.VMEM(scales_shape, bf16),
        ],
        in_specs=[in_vmem] * count + [anywhere, in_vmem][: len(begun)],
        out_specs=[anywhere, in_vmem],
        input_output_aliases={count: 0} if begun else {},
        scratch_shapes=[pltpu.SemaphoreType.DMA((count,))],
        compiler_params=pltpu.CompilerParams(vmem_limit_bytes=8 * MIB),
        cost_estimate=pl.CostEstimate(flops=0, bytes_accessed=1, transcendentals=0),
        name="lay",
    )(*[vmem(s) for s in shards], *begun)


def shards(grad_values, grad_exponents, proj, weights, moment1, moment2):
    grid = Grid()
    size = grid.size
    values, exponents = grad_values[0], grad_exponents[0]
    width, columns = values.shape
    nblocks = exponents.shape[0]
    blocksize = columns // nblocks
    rows = width // grid.nodes // size["y"]
    ranks = proj.shape[1]
    pieces = []
    for block, blocks, half, halves in PIECES:
        n, m = rows // halves, columns // blocks
        pieces.append((slice(half * n, (half + 1) * n), slice(block * m, (block + 1) * m)))

    other = dequant(grid, values, exponents, 1, rows, blocksize, pieces) if size["c"] > 1 else []
    other = [grid.send(t, c=1) for t in other]
    mine = dequant(grid, values, exponents, 0, rows, blocksize, pieces)
    units = [Unit(grid, list(terms)) for terms in zip(mine, *([other] if other else []))]
    for turn in range(3):
        for unit, order in zip(units, ORDERS):
            unit.hop(order[turn])

    packs = [pack(proj, [moment1, moment2])]
    packs += [grid.send(packs[0], v=-d) for d in grid.others("v")]

    parts, projected = project(grid, units, pieces, packs, rows, ranks, columns)
    received = [grid.send(t, v=d) for d, t in zip(grid.others("v"), parts[1:])]

    terms = [projected[0]] + [grid.send(projected[d], c=d) for d in grid.others("c")]
    by_x = add_cut(terms, "add_cores")
    by_y = []
    for dy in range(size["y"]):
        for dx in range(size["x"]):
            by_y.append(grid.send(by_x[dx], x=dx, y=dy) if dx or dy else by_x[0])
    if size["y"] > 2:
        stacked = jnp.stack(by_y).reshape((size["y"], -1) + by_y[0].shape)
        came = jnp.stack([grid.step("y", grid.place()["y"], -d) for d in range(size["y"])])
        order = jnp.zeros(size["y"], jnp.int32).at[came].set(jnp.arange(size["y"], dtype=jnp.int32))
        stacked = jnp.take(stacked, order, axis=0)
        by_y = [stacked[i, j] for i in range(size["y"]) for j in range(stacked.shape[1])]
    by_w = add_cut(by_y, "add_chips", size["x"])
    summed = [
        grid.send(by_w[dw], w=dw, v=dv) if dw or dv else by_w[0]
        for dv in range(size["v"])
        for dw in range(size["w"])
    ]
    added, kept = normalize(grid, summed, packs, rows, 0, columns)
    added = add([added] + [grid.send(added, c=d) for d in grid.others("c")], "add_sums", f32)
    sums = [
        grid.send(added, x=dx, w=dw) if dx or dw else added
        for dx in range(size["x"])
        for dw in range(size["w"])
    ]
    new, new1, new2, packed = update(
        weights, [moment1, moment2], [parts[0], *received], sums, kept, blocksize
    )

    along_v = [packed] + [grid.send(packed, v=d) for d in grid.others("v")]
    held = []
    for dv, over_v in enumerate(along_v):
        along_w = [over_v] + [grid.send(over_v, w=d) for d in grid.others("w")]
        for dw, over_w in enumerate(along_w):
            along_x = [over_w] + [grid.send(over_w, x=d) for d in grid.others("x")]
            for dx, over_x in enumerate(along_x):
                along_c = [over_x] + [grid.send(over_x, c=d) for d in grid.others("c")]
                for dc, shard in enumerate(along_c):
                    held.append((shard, {"v": dv, "w": dw, "x": dx, "c": dc}))
    late = [t for t in held if t[1]["v"] and t[1]["w"]]
    if late and rows % 128 == 0:
        early = [t for t in held if not (t[1]["v"] and t[1]["w"])]
        begun = lay(grid, early, nblocks)
        quant, scales = lay(grid, late, nblocks, *begun)
    else:
        quant, scales = lay(grid, held, nblocks)
    return quant, scales, new, new1, new2


def solution(mesh):
    return jax.shard_map(
        shards,
        mesh=mesh,
        in_specs=(
            P(("node", "local"), None, None),
            P(("node", "local"), None, None),
            P(("local", "node"), None),
            P(("local", "node"), None),
            P("node", None),
            P("node", None),
        ),
        out_specs=(
            P("local", None),
            P(None, "local"),
            P(("local", "node"), None),
            P("node", None),
            P("node", None),
        ),
        check_vma=False,
    )
```
